128 devices in a mesh: layer: 8 (over x, z_hi), seq: 16 (over z_lo, y, core).
Axes of the slice: x: 4, y: 4, z: 4 (z_hi: 2, z_lo: 2; z = z_hi * 2 + z_lo), core: 2. Of those that a mesh axis runs over, the one named last changes fastest.
Arguments:
- panels: bfloat16 [8, 2560, 2048], P('layer', 'seq'), may hold values from -6 to 6
- feed: bfloat16 [2, 2560, 2048], P(None, 'seq'), may hold values from -6 to 6
- ssm_state: float32 [8, 16, 64, 64, 128], P('layer', 'seq'), may hold values from -6 to 6
- conv_state: bfloat16 [8, 16, 3, 5120], P('layer', 'seq'), may hold values from -6 to 6
- w_in: bfloat16 [8, 2048, 9280], P('layer', 'seq'), may hold values from -0.125 to 0.125
- w_out: bfloat16 [8, 4096, 2048], P('layer'), may hold values from -0.09375 to 0.09375
- norm_gain: float32 [8, 2048], P('layer'), may hold values from 0.25 to 1.75
- conv_weight: float32 [8, 4, 5120], P('layer'), may hold values from -3 to 3
- conv_bias: float32 [8, 5120], P('layer'), may hold values from -3 to 3
- dt_bias: float32 [8, 64], P('layer'), may hold values from -3 to 0
- decay_rate: float32 [8, 64], P('layer'), may hold values from 0.01 to 2
- skip_gain: float32 [8, 64], P('layer'), may hold values from 0.5 to 2
- out_gain: float32 [8, 4096], P('layer'), may hold values from 0.25 to 1.75
Outputs:
- panels_out: bfloat16 [8, 2560, 2048], P('layer', 'seq')
- states_out: float32 [8, 16, 64, 64, 128], P('layer', 'seq')
The draws below stay inside these ranges and needn't reach their ends.
All inputs are finite; a program needn't handle non-finite values.
Results may differ from the reference program's by a relative error of at most 0.015.
Values may be sent and summed in bfloat16 or wider, within the bound.
A program may use at most 192 MiB of HBM per device.

```python
import math
import jax
import jax.numpy as jnp
from jax import lax

WIDTH = 2048
HEADS = 64
HEAD_DIM = 64
STATE = 128
GROUPS = 4
KERNEL = 4
SEGMENT = 160
TURNS = 3
INNER = 4096
CONV_CH = 5120
PROJ = 9280
TOKENS = 2560
N_LAYER = 8
N_SEQ = 16


def block_scale(key, dims, pieces, least, high):
    loudness = 1.0
    for dim, shards_of in pieces:
        steps = jax.random.uniform(jax.random.fold_in(jax.random.fold_in(key, 6), dim), (shards_of,), jnp.float32, least / len(pieces), high / len(pieces))
        loudness = loudness * jnp.repeat(jnp.exp(steps), dims[dim] // shards_of).reshape((-1,) + (1,) * (len(dims) - 1 - dim))
    return loudness


def scatter_about(stream_key, shape, spread, limit, cuts=(), held_as=jnp.bfloat16):
    drawn = spread * jax.random.normal(stream_key, shape, jnp.float32)
    if cuts:
        drawn = drawn * block_scale(stream_key, shape, cuts, -0.22, 0.18)
    return jnp.clip(drawn, -limit, limit).astype(held_as)


def setup_inputs(seed: int = 0) -> dict:
    streams_of = jax.random.split(jax.random.key(seed), 14)
    return {
        "panels": scatter_about(streams_of[0], (N_LAYER, TOKENS, WIDTH), 1.0, 6.0, ((0, 8), (1, 16))),
        "feed": scatter_about(streams_of[1], (TURNS - 1, TOKENS, WIDTH), 1.0, 6.0, ((1, 16),)),
        "ssm_state": scatter_about(streams_of[2], (N_LAYER, N_SEQ, HEADS, HEAD_DIM, STATE), 1.0, 6.0, ((0, 8), (1, 16)), jnp.float32),
        "conv_state": scatter_about(streams_of[3], (N_LAYER, N_SEQ, KERNEL - 1, CONV_CH), 1.0, 6.0, ((0, 8), (1, 16))),
        "w_in": scatter_about(streams_of[4], (N_LAYER, WIDTH, PROJ), WIDTH ** -0.5, 0.125, ((0, 8), (1, 16))),
        "w_out": scatter_about(streams_of[5], (N_LAYER, INNER, WIDTH), INNER ** -0.5, 0.09375, ((0, 8),)),
        "norm_gain": jnp.clip(1.0 + 0.15 * jax.random.normal(streams_of[6], (N_LAYER, WIDTH), jnp.float32), 0.25, 1.75),
        "conv_weight": scatter_about(streams_of[7], (N_LAYER, KERNEL, CONV_CH), KERNEL ** -0.5, 3.0, ((0, 8),), jnp.float32),
        "conv_bias": scatter_about(streams_of[8], (N_LAYER, CONV_CH), 0.5, 3.0, ((0, 8),), jnp.float32),
        "dt_bias": jnp.clip(-3.0 + 3.0 * jax.random.uniform(streams_of[9], (N_LAYER, HEADS), jnp.float32) ** block_scale(streams_of[9], (N_LAYER, HEADS), ((0, 8),), -0.2, 0.2), -3.0, 0.0),
        "decay_rate": jnp.clip(jnp.exp(math.log(2.0) - 5.2983174 * jax.random.uniform(streams_of[10], (N_LAYER, HEADS), jnp.float32) ** block_scale(streams_of[10], (N_LAYER, HEADS), ((0, 8),), -0.2, 0.2)), 0.01, 2.0),
        "skip_gain": jnp.clip(0.5 + 1.5 * jax.random.uniform(streams_of[11], (N_LAYER, HEADS), jnp.float32) ** block_scale(streams_of[11], (N_LAYER, HEADS), ((0, 8),), -0.2, 0.2), 0.5, 2.0),
        "out_gain": jnp.clip(1.0 + 0.15 * jax.random.normal(streams_of[12], (N_LAYER, INNER), jnp.float32), 0.25, 1.75),
    }


EPS = 1e-05

def rms_scale(values, gain):
    return values * lax.rsqrt(lax.optimization_barrier(jnp.mean(values * values, axis=-1, keepdims=True)) + EPS) * gain

def mixer_core(projected, state_now, tail_now, conv_weight, conv_bias, dt_bias, decay_rate, skip_gain, out_gain):
    row_count = projected.shape[0]
    per_group = HEADS // GROUPS
    highest = lax.Precision.HIGHEST
    gate_branch = projected[:, :INNER]
    conv_input = projected[:, INNER:INNER + CONV_CH].astype(jnp.bfloat16)
    step_logit = projected[:, INNER + CONV_CH:]
    window = jnp.concatenate([tail_now, conv_input], axis=0)
    conv_sum = jnp.zeros((row_count, CONV_CH), jnp.float32)
    for offset in range(KERNEL):
        conv_sum = conv_sum + window[offset:offset + row_count].astype(jnp.float32) * conv_weight[offset]
    activated = jax.nn.silu(conv_sum + conv_bias)
    ssm_input = activated[:, :INNER].astype(jnp.bfloat16).reshape(row_count, GROUPS, per_group, HEAD_DIM)
    write_map = activated[:, INNER:INNER + GROUPS * STATE].astype(jnp.bfloat16).reshape(row_count, GROUPS, STATE)
    read_map = activated[:, INNER + GROUPS * STATE:].astype(jnp.bfloat16).reshape(row_count, GROUPS, STATE)
    step_size = jax.nn.softplus(step_logit + dt_bias)
    log_decay = jnp.cumsum(-decay_rate * step_size, axis=0)
    head_decay = log_decay.T
    causal = jnp.arange(row_count)[:, None] >= jnp.arange(row_count)[None, :]
    decay_gap = head_decay[:, :, None] - head_decay[:, None, :]
    decay_mask = jnp.where(causal, jnp.exp(jnp.where(causal, decay_gap, 0.0)), 0.0)
    read_wide = read_map.astype(jnp.float32)
    write_wide = write_map.astype(jnp.float32)
    input_wide = ssm_input.astype(jnp.float32)
    scores = jnp.einsum('tgn,sgn->gts', read_wide, write_wide, precision=highest)
    weights = (scores[:, None] * decay_mask.reshape(GROUPS, per_group, row_count, row_count) * step_size.T.reshape(GROUPS, per_group, 1, row_count)).astype(jnp.bfloat16)
    local_out = jnp.einsum('ghts,sghp->tghp', weights.astype(jnp.float32), input_wide, precision=highest)
    state_view = state_now.reshape(GROUPS, per_group, HEAD_DIM, STATE)
    carried = jnp.einsum('tgn,ghpn->tghp', read_wide, state_view, precision=highest)
    carried = carried * jnp.exp(log_decay).reshape(row_count, GROUPS, per_group, 1)
    combined = local_out + carried + skip_gain.reshape(GROUPS, per_group, 1) * input_wide
    gated = combined.reshape(row_count, INNER) * jax.nn.silu(gate_branch)
    mixed_norm = rms_scale(gated, out_gain).astype(jnp.bfloat16)
    final_decay = log_decay[-1]
    end_weight = jnp.exp(final_decay[None, :] - log_decay) * step_size
    scaled_input = input_wide * end_weight.reshape(row_count, GROUPS, per_group, 1)
    new_state = jnp.exp(final_decay).reshape(GROUPS, per_group, 1, 1) * state_view
    new_state = new_state + jnp.einsum('sghp,sgn->ghpn', scaled_input, write_wide, precision=highest)
    return (mixed_norm, new_state.reshape(HEADS, HEAD_DIM, STATE), conv_input[row_count - (KERNEL - 1):])

def run_tile(panel_now, state_now, tail_now, params):
    w_in, w_out, norm_gain, conv_weight, conv_bias, dt_bias, decay_rate, skip_gain, out_gain = params
    normed = rms_scale(panel_now.astype(jnp.float32), norm_gain).astype(jnp.bfloat16)
    projected = jnp.dot(normed, w_in, preferred_element_type=jnp.float32)
    mixed_norm, new_state, new_tail = mixer_core(projected, state_now, tail_now, conv_weight, conv_bias, dt_bias, decay_rate, skip_gain, out_gain)
    panel_out = (panel_now.astype(jnp.float32) + jnp.dot(mixed_norm, w_out, preferred_element_type=jnp.float32)).astype(jnp.bfloat16)
    return (panel_out, new_state, new_tail)

def section_step(pack):
    return jax.vmap(run_tile, in_axes=(0, 0, 0, None))(pack[0], pack[1], pack[2], pack[3:])

def reference(panels, feed, ssm_state, conv_state, w_in, w_out, norm_gain, conv_weight, conv_bias, dt_bias, decay_rate, skip_gain, out_gain):
    current = panels.reshape(N_LAYER, N_SEQ, SEGMENT, WIDTH)
    states = ssm_state
    conv_tails = conv_state
    for step_index in range(TURNS):
        panel_out, state_out, tail_out = lax.map(section_step, (current, states, conv_tails, w_in, w_out, norm_gain, conv_weight, conv_bias, dt_bias, decay_rate, skip_gain, out_gain))
        if step_index + 1 < TURNS:
            fresh_rows = feed[step_index].reshape(1, N_SEQ, SEGMENT, WIDTH)
            current = jnp.concatenate([fresh_rows, panel_out[:-1]], axis=0)
            states = jnp.concatenate([jnp.zeros_like(state_out[:, :1]), state_out[:, :-1]], axis=1)
            conv_tails = jnp.concatenate([jnp.zeros_like(tail_out[:, :1]), tail_out[:, :-1]], axis=1)
    return (panel_out.reshape(N_LAYER, TOKENS, WIDTH), state_out)
```

```python
import functools

import jax
import jax.numpy as jnp
from jax import lax
from jax.experimental import pallas as pl
from jax.experimental.pallas import tpu as pltpu
from jax.sharding import PartitionSpec as P

EPS = 1e-05
F32 = jnp.float32
BF16 = jnp.bfloat16
SEG = 160
WIDTH = 2048
HALF = 2048
CHUNK = 256
STEPS = HALF // CHUNK
PIECE = 512
PIECES = WIDTH // PIECE
MESH = pl.DeviceIdType.MESH
HIGHEST = lax.Precision.HIGHEST


def silu(v):
    half = 0.5 * v
    return half + half * jnp.tanh(half)


def dot(a, b):
    return jnp.dot(a, b, preferred_element_type=F32)


def by_rows(v, scale):
    blocks = [v[:, i : i + 128] * scale for i in range(0, v.shape[1], 128)]
    return blocks[0] if len(blocks) == 1 else jnp.concatenate(blocks, axis=1)


def lane_sums(v):
    total = v[:, :128]
    for i in range(128, v.shape[1], 128):
        total = total + v[:, i : i + 128]
    return total


def kernel(
    panels, feed, state_in, tail_in, w_in, w_dt, w_out, norm_gain, conv_w, conv_b, heads, skip, out_gain,
    panel_out, state_out,
    w_main, w_bc, w_o, hid, hg, ssq, rowscale, tails, s_in, s_loc, s_send, s_recv, s_stage, fd,
    convbuf, proj, b_all, c_all, score_a, score_b, ld_col, ld_row, st_row, e_ld, e_end, e_fin,
    gated, own_part, part_send, part_recv, sq_mine, sq_send, sq_recv, pan_send,
    g_send, g_recv, g_loc, l_sem, m_send, m_recv, p_send, p_recv, n_send, n_recv, r_send, r_recv,
    st_send, st_recv, f_send, f_recv, f_loc,
):
    layer = lax.axis_index("layer")
    seq = lax.axis_index("seq")
    c = lax.rem(seq, 2)
    m = lax.div(seq, 2)
    y = lax.rem(m, 4)
    z = lax.div(m, 4)
    oc = 1 - c
    yp = lax.rem(y + 1, 4)
    ym = lax.rem(y + 3, 4)
    y2 = lax.rem(y + 2, 4)
    oz = 1 - z

    def at(zz, yy, cc):
        return (layer, zz * 8 + yy * 2 + cc)

    sib = at(z, y, oc)
    to_yp = at(z, yp, c)
    to_ym = at(z, ym, c)
    to_z = at(oz, y, c)
    up = (lax.rem(layer + 1, 8), seq)
    down = (lax.rem(layer + 7, 8), seq)
    after = (layer, lax.rem(seq + 2, 16))
    before = (layer, lax.rem(seq + 14, 16))

    barrier = pltpu.get_barrier_semaphore()
    friends = (sib, to_yp, to_ym, to_z, up, down, after, before)
    for friend in friends:
        pl.semaphore_signal(barrier, inc=1, device_id=friend, device_id_type=MESH)
    pl.semaphore_wait(barrier, len(friends))

    def remote(src, dst, ss, rs, who):
        return pltpu.make_async_remote_copy(
            src_ref=src, dst_ref=dst, send_sem=ss, recv_sem=rs, device_id=who, device_id_type=MESH
        )

    def mult(v, by):
        return pl.multiple_of(v, by)

    own_rows = mult(m * 256 + c * 128, 128)
    sib_rows = mult(m * 256 + oc * 128, 128)

    def bc_first(cc):
        rows = pl.ds(own_rows, 128)
        return (
            (w_in.at[:, pl.ds(mult(8192 + cc * 256, 128), 256)], w_bc.at[rows, pl.ds(0, 256)]),
            (w_in.at[:, pl.ds(mult(8704 + cc * 256, 128), 256)], w_bc.at[rows, pl.ds(256, 256)]),
            (w_dt, w_bc.at[rows, pl.ds(512, 128)]),
        )

    def bc_landed():
        rows = pl.ds(sib_rows, 128)
        return (
            w_bc.at[rows, pl.ds(0, 256)],
            w_bc.at[rows, pl.ds(256, 256)],
            w_bc.at[rows, pl.ds(512, 128)],
        )

    bc_slots = (18, 19, 3)

    def main_first(q, cc):
        rows = pl.ds(own_rows, 128)
        return (
            (w_in.at[:, pl.ds(mult(4096 + cc * 2048 + q * 256, 128), 256)], w_main.at[q, rows, pl.ds(0, 256)]),
            (w_in.at[:, pl.ds(mult(cc * 2048 + q * 256, 128), 256)], w_main.at[q, rows, pl.ds(256, 256)]),
        )

    def main_landed(q):
        rows = pl.ds(sib_rows, 128)
        return (w_main.at[q, rows, pl.ds(0, 256)], w_main.at[q, rows, pl.ds(256, 256)])

    for (src, dst), slot in zip(bc_first(oc), bc_slots):
        remote(src, dst, g_send.at[8, slot], g_recv.at[8, slot], sib).start()
    for i, (src, dst) in enumerate(bc_first(c)):
        pltpu.make_async_copy(src, dst, g_loc.at[8, i]).start()

    @pl.loop(0, STEPS)
    def _(q):
        for i, (src, dst) in enumerate(main_first(q, oc)):
            remote(src, dst, g_send.at[q, 18 + i], g_recv.at[q, 18 + i], sib).start()
        for i, (src, dst) in enumerate(main_first(q, c)):
            pltpu.make_async_copy(src, dst, g_loc.at[q, i]).start()

    def bc_part(mm, half=None):
        if half is None:
            return w_bc.at[pl.ds(mult(mm * 256, 256), 256), :]
        return w_bc.at[pl.ds(mult(mm * 256 + half * 128, 128), 128), :]

    def x_part(q, mm, half=None):
        if half is None:
            return w_main.at[q, pl.ds(mult(mm * 256, 256), 256), pl.ds(0, 256)]
        return w_main.at[q, pl.ds(mult(mm * 256 + half * 128, 128), 128), pl.ds(0, 256)]

    def g_part(q, mm, half=None):
        if half is None:
            return w_main.at[q, pl.ds(mult(mm * 256, 256), 256), pl.ds(256, 256)]
        return w_main.at[q, pl.ds(mult(mm * 256 + half * 128, 128), 128), pl.ds(256, 256)]

    m_yp, m_ym, m_y2 = z * 4 + yp, z * 4 + ym, z * 4 + y2
    o_y, o_yp, o_ym, o_y2 = oz * 4 + y, oz * 4 + yp, oz * 4 + ym, oz * 4 + y2

    def push(part, q, slot, who):
        remote(part, part, g_send.at[q, slot], g_recv.at[q, slot], who).start()

    def arrived(part, q, slot):
        remote(part, part, g_send.at[q, slot], g_recv.at[q, slot], sib).wait_recv()

    def sent(part, q, slot):
        remote(part, part, g_send.at[q, slot], g_recv.at[q, slot], sib).wait_send()

    def first_x(part, q):
        push(part(m), q, 2, to_z)
        push(part(m), q, 0, to_yp)
        push(part(m), q, 1, to_ym)

    def first_g(part, q):
        push(part(m), q, 5, to_z)
        push(part(m), q, 3, to_yp)
        push(part(m), q, 4, to_ym)

    def second_x(part, q):
        arrived(part(o_y), q, 2)
        push(part(o_y), q, 6, to_yp)
        push(part(o_y), q, 7, to_ym)
        arrived(part(m_ym), q, 0)
        push(part(m_ym, 0), q, 8, to_yp)
        arrived(part(m_yp), q, 1)
        push(part(m_yp, 1), q, 9, to_ym)

    def second_g(part, q):
        arrived(part(m_ym), q, 3)
        push(part(m_ym), q, 11, to_z)
        push(part(m_ym, 0), q, 10, to_yp)
        arrived(part(m_yp), q, 4)
        push(part(m_yp), q, 13, to_z)
        push(part(m_yp, 1), q, 12, to_ym)
        arrived(part(o_y), q, 5)

    def third_x(part, q):
        arrived(part(o_ym), q, 6)
        push(part(o_ym, 0), q, 14, to_yp)
        arrived(part(o_yp), q, 7)
        push(part(o_yp, 1), q, 15, to_ym)
        arrived(part(m_y2, 0), q, 8)
        arrived(part(m_y2, 1), q, 9)

    def third_g(part, q):
        arrived(part(m_y2, 0), q, 10)
        push(part(m_y2, 0), q, 16, to_z)
        arrived(part(m_y2, 1), q, 12)
        push(part(m_y2, 1), q, 17, to_z)
        arrived(part(o_ym), q, 11)
        arrived(part(o_yp), q, 13)

    def last_x(part, q):
        arrived(part(o_y2, 0), q, 14)
        arrived(part(o_y2, 1), q, 15)

    def last_g(part, q):
        arrived(part(o_y2, 0), q, 16)
        arrived(part(o_y2, 1), q, 17)

    def sent_x(part, q):
        for slot in (0, 1, 2, 6, 7):
            sent(part(m), q, slot)
        for slot in (8, 9, 14, 15):
            sent(part(m, 0), q, slot)

    def sent_g(part, q):
        for slot in (3, 4, 5, 11, 13):
            sent(part(m), q, slot)
        for slot in (10, 12, 16, 17):
            sent(part(m, 0), q, slot)

    for (src, dst), slot, i in zip(bc_first(c), bc_slots, range(3)):
        pltpu.make_async_copy(src, dst, g_loc.at[8, i]).wait()
    for dst, slot in zip(bc_landed(), bc_slots):
        arrived(dst, 8, slot)
    first_x(bc_part, 8)

    @pl.loop(0, STEPS)
    def _(q):
        for i, (src, dst) in enumerate(main_first(q, c)):
            pltpu.make_async_copy(src, dst, g_loc.at[q, i]).wait()
        for i, dst in enumerate(main_landed(q)):
            arrived(dst, q, 18 + i)
        first_x(functools.partial(x_part, q), q)
        first_g(functools.partial(g_part, q), q)

    begin = (
        (panels, hid.at[0, c], 0),
        (tail_in, tails.at[0, c], 1),
        (state_in.at[pl.ds(mult(oc * HALF, HALF), HALF), :], s_in.at[c], 2),
    )
    for src, dst, i in begin:
        remote(src, dst, m_send.at[i], m_recv.at[i], sib).start()
    local = (
        (panels, hid.at[0, c]),
        (tail_in, tails.at[0, c]),
        (state_in.at[pl.ds(mult(c * HALF, HALF), HALF), :], s_in.at[c]),
        (w_out.at[pl.ds(mult(c * HALF, HALF), HALF), :], w_o),
        (feed, fd),
    )
    for i, (src, dst) in enumerate(local):
        pltpu.make_async_copy(src, dst, l_sem.at[i]).start()
    for i, (src, dst) in enumerate(local):
        pltpu.make_async_copy(src, dst, l_sem.at[i]).wait()
    for (src, dst, i), land in zip(begin, (hid.at[0, oc], tails.at[0, oc], s_in.at[oc])):
        remote(land, land, m_send.at[i], m_recv.at[i], sib).wait_recv()

    def ingest(t, tile, n):
        cols = pl.ds(mult(n * PIECE, PIECE), PIECE)
        rows = pl.ds(mult(tile * SEG, 32), SEG)
        h = hid[t, tile, :, cols].astype(F32)
        ssq[rows, :] += lane_sums(h * h)
        hg[rows, cols] = (h * norm_gain[:, cols]).astype(BF16)

    lane = lax.broadcasted_iota(jnp.int32, (SEG, 128), 1)
    row = lax.broadcasted_iota(jnp.int32, (SEG, 128), 0)

    def conv(width, tile_tail, fresh, weight, bias):
        convbuf[0:8, 0:width] = tile_tail
        convbuf[8 : 8 + SEG, 0:width] = fresh
        total = bias
        for k in range(4):
            total = total + convbuf[5 + k : 5 + k + SEG, 0:width] * weight[k : k + 1, :]
        return silu(total).astype(BF16)

    def tail_of(t, tile, cols):
        value = tails[t, tile, :, cols]
        if t > 0 and tile == 0:
            value = jnp.where(m > 0, value, 0.0)
        return value

    def keep_tail(t, tile, cols, width):
        if t < 2:
            tails[t + 1, 1 if tile == 0 else 2, :, cols] = convbuf[SEG : SEG + 8, 0:width]

    def prologue(t):
        total = jnp.sum(ssq[...], axis=1, keepdims=True)
        rowscale[...] = jnp.broadcast_to(lax.rsqrt(total * (1.0 / WIDTH) + EPS), (2 * SEG, 128))
        proj[:, 0:512] = dot(hg[...], w_bc[:, 0:512])
        logits = dot(hg[...], w_bc[:, 512:640])
        causal = lane <= row
        tri = (
            lax.broadcasted_iota(jnp.int32, (SEG, SEG), 1) <= lax.broadcasted_iota(jnp.int32, (SEG, SEG), 0)
        ).astype(F32)
        for tile in range(2):
            rows = slice(tile * SEG, (tile + 1) * SEG)
            scale = rowscale[rows, :]
            for which, base in ((0, 4096), (1, 4608)):
                cols = pl.ds(mult(base + c * 256, 128), 256)
                fresh = by_rows(proj[rows, which * 256 : which * 256 + 256], scale).astype(BF16).astype(F32)
                made = conv(256, tail_of(t, tile, cols), fresh, conv_w[:, cols], conv_b[:, cols])
                keep_tail(t, tile, cols, 256)
                target = b_all if which == 0 else c_all
                target[tile, 0] = made[:, 0:128]
                target[tile, 1] = made[:, 128:256]
            for g in range(2):
                scores = lax.dot_general(
                    c_all[tile, g], b_all[tile, g], (((1,), (1,)), ((), ())), preferred_element_type=F32
                )
                score_a[tile, g] = jnp.where(causal, scores[:, 0:128], 0.0)
                score_b[tile, g] = jnp.where(causal[0:32, 0:32], scores[128:SEG, 128:SEG], 0.0)
            v = logits[rows, :] * scale + heads[0:1, :]
            step = jnp.maximum(v, 0.0) + jnp.log1p(jnp.exp(-jnp.abs(v)))
            ld = jnp.dot(tri, -heads[1:2, :] * step, preferred_element_type=F32, precision=HIGHEST)
            last = ld[SEG - 1 : SEG, :]
            ld_col[tile] = ld
            ld_row[tile, :, 0:SEG] = ld.T
            st_row[tile, :, 0:SEG] = step.T
            e_ld[tile] = jnp.exp(ld).astype(BF16)
            e_end[tile] = (jnp.exp(last - ld) * step).astype(BF16)
            e_fin[tile] = jnp.broadcast_to(jnp.exp(last), (8, 128))

    def step_of(t, q):
        g = lax.div(q, 4)
        base = c * 32 + q * 4
        cols = pl.ds(mult(c * HALF + q * CHUNK, CHUNK), CHUNK)
        proj[...] = dot(hg[...], w_main[q])
        spread = (
            lax.broadcasted_iota(jnp.int32, (128, CHUNK), 0)
            == base + lax.div(lax.broadcasted_iota(jnp.int32, (128, CHUNK), 1), 64)
        ).astype(F32)
        spread16 = spread.astype(BF16)
        weight, bias = conv_w[:, cols], conv_b[:, cols]
        skip_now, gain_now = skip[:, cols], out_gain[:, cols]
        if t > 0:
            remote(s_recv.at[t - 1, q], s_recv.at[t - 1, q], st_send.at[t - 1, q], st_recv.at[t - 1, q], after).wait_recv()
        made = []
        for tile in range(2):
            rows = slice(tile * SEG, (tile + 1) * SEG)
            scale = rowscale[rows, :]
            fresh = by_rows(proj[rows, 0:CHUNK], scale).astype(BF16).astype(F32)
            x = conv(CHUNK, tail_of(t, tile, cols), fresh, weight, bias)
            keep_tail(t, tile, cols, CHUNK)
            if t == 0:
                state = s_in[tile, pl.ds(mult(q * CHUNK, CHUNK), CHUNK), :].T
            elif tile == 0:
                state = jnp.where(m > 0, s_recv[t - 1, q].astype(F32), 0.0)
            else:
                state = s_loc[q]
            ld = pltpu.roll(ld_col[tile], lax.rem(128 - base, 128), 1)
            sa, sb = score_a[tile, g], score_b[tile, g]
            pairs = []
            for pair in range(2):
                xp = x[:, pair * 128 : pair * 128 + 128]
                outs = []
                for i in range(2):
                    h = pair * 2 + i
                    col = jnp.broadcast_to(ld[:, h : h + 1], (SEG, 128))
                    ldr = ld_row[tile, pl.ds(base + h, 1), :]
                    str_ = st_row[tile, pl.ds(base + h, 1), :]
                    wa = sa * jnp.exp(jnp.minimum(col - ldr[:, 0:128], 0.0)) * str_[:, 0:128]
                    wb = sb * jnp.exp(jnp.minimum(col[128:SEG, 0:32] - ldr[:, 128:SEG], 0.0)) * str_[:, 128:SEG]
                    oa = dot(wa.astype(BF16), xp[0:128])
                    ob = dot(wb.astype(BF16), xp[128:SEG])
                    outs.append(jnp.concatenate([oa[0:128], oa[128:SEG] + ob], axis=0))
                pairs.append(jnp.where(lane < 64, outs[0], outs[1]))
            mixed = jnp.concatenate(pairs, axis=1)
            carried = dot(c_all[tile, g], state.astype(BF16)) * dot(e_ld[tile], spread16)
            wide = x.astype(F32)
            combined = mixed + carried + skip_now * wide
            out = combined * silu(by_rows(proj[rows, CHUNK : 2 * CHUNK], scale))
            sq_mine[rows, :] += lane_sums(out * out)
            gated[rows, pl.ds(mult(q * CHUNK, CHUNK), CHUNK)] = (out * gain_now).astype(BF16)
            scaled = (wide * dot(e_end[tile], spread16)).astype(BF16)
            grown = lax.dot_general(
                b_all[tile, g], scaled, (((0,), (0,)), ((), ())), preferred_element_type=F32
            )
            fade = jnp.dot(e_fin[tile], spread, preferred_element_type=F32, precision=HIGHEST)
            made.append(fade[0:1, :] * state + grown)
        if t < 2:
            s_loc[q] = made[0]
            s_send[t, q] = made[1].astype(BF16)
            remote(s_send.at[t, q], s_recv.at[t, q], st_send.at[t, q], st_recv.at[t, q], after).start()
        else:
            s_stage[0, q] = made[0].T
            s_stage[1, q] = made[1].T
            place = state_out.at[pl.ds(mult(c * HALF + q * CHUNK, CHUNK), CHUNK), :]
            pltpu.make_async_copy(s_stage.at[c, q], place, f_loc.at[q]).start()
            remote(s_stage.at[oc, q], place, f_send.at[q], f_recv.at[q], sib).start()

    own = pl.ds(mult(c * SEG, 32), SEG)
    other = pl.ds(mult(oc * SEG, 32), SEG)

    def project_out(t, n):
        cols = pl.ds(mult(n * PIECE, PIECE), PIECE)
        proj[...] = dot(gated[...], w_o[:, cols])
        part_send[t, n] = proj[other, :].astype(BF16)
        own_part[n] = proj[own, :]
        remote(part_send.at[t, n], part_recv.at[t, n], p_send.at[t, n], p_recv.at[t, n], sib).start()

    def finish(t, n, scale):
        cols = pl.ds(mult(n * PIECE, PIECE), PIECE)
        remote(part_recv.at[t, n], part_recv.at[t, n], p_send.at[t, n], p_recv.at[t, n], sib).wait_recv()
        whole = own_part[n] + part_recv[t, n].astype(F32)
        panel = (hid[t, c, :, cols].astype(F32) + by_rows(whole, scale)).astype(BF16)
        if t < 2:
            pan_send[t, :, cols] = jnp.where(layer == 7, fd[t, :, cols].astype(F32), panel.astype(F32)).astype(BF16)
            remote(
                pan_send.at[t, :, cols], hid.at[t + 1, c, :, cols], n_send.at[t, n], n_recv.at[t, n], up
            ).start()
        else:
            panel_out[:, cols] = panel

    for t in range(3):
        ssq[...] = jnp.zeros((2 * SEG, 128), F32)
        sq_mine[...] = jnp.zeros((2 * SEG, 128), F32)
        if t == 0:

            @pl.loop(0, 2 * PIECES)
            def _(i):
                ingest(0, lax.rem(i, 2), lax.div(i, 2))

            second_x(bc_part, 8)

            @pl.loop(0, STEPS)
            def _(q):
                second_x(functools.partial(x_part, q), q)
                second_g(functools.partial(g_part, q), q)

            third_x(bc_part, 8)

            @pl.loop(0, STEPS)
            def _(q):
                third_x(functools.partial(x_part, q), q)
                third_g(functools.partial(g_part, q), q)

            last_x(bc_part, 8)
        else:

            @pl.loop(0, PIECES)
            def _(n):
                part = hid.at[t, c, :, pl.ds(mult(n * PIECE, PIECE), PIECE)]
                remote(part, part, n_send.at[t - 1, n], n_recv.at[t - 1, n], up).wait_recv()
                remote(part, part, r_send.at[t - 1, n], r_recv.at[t - 1, n], sib).start()
                ingest(t, c, n)

            @pl.loop(0, PIECES)
            def _(n):
                part = hid.at[t, oc, :, pl.ds(mult(n * PIECE, PIECE), PIECE)]
                remote(part, part, r_send.at[t - 1, n], r_recv.at[t - 1, n], sib).wait_recv()
                ingest(t, oc, n)

            remote(tails.at[t, 0], tails.at[t, 0], m_send.at[2 + t], m_recv.at[2 + t], after).wait_recv()
        prologue(t)

        @pl.loop(0, STEPS)
        def _(q):
            if t == 0:
                last_x(functools.partial(x_part, q), q)
                last_g(functools.partial(g_part, q), q)
            step_of(t, q)

        if t < 2:
            remote(tails.at[t + 1, 2], tails.at[t + 1, 0], m_send.at[3 + t], m_recv.at[3 + t], after).start()
        sq_send[t] = sq_mine[other, :]
        remote(sq_send.at[t], sq_recv.at[t], m_send.at[5 + t], m_recv.at[5 + t], sib).start()
        project_out(t, 0)
        remote(sq_recv.at[t], sq_recv.at[t], m_send.at[5 + t], m_recv.at[5 + t], sib).wait_recv()
        squares = jnp.sum(sq_mine[own, :] + sq_recv[t], axis=1, keepdims=True)
        rowscale[0:SEG, :] = jnp.broadcast_to(lax.rsqrt(squares * (1.0 / 4096) + EPS), (SEG, 128))

        @pl.loop(1, PIECES)
        def _(n):
            project_out(t, n)
            finish(t, n - 1, rowscale[0:SEG, :])

        finish(t, PIECES - 1, rowscale[0:SEG, :])

    for i, slot in enumerate(bc_slots):
        sent(bc_landed()[i], 8, slot)
    sent_x(bc_part, 8)

    @pl.loop(0, STEPS)
    def _(q):
        for i, dst in enumerate(main_landed(q)):
            sent(dst, q, 18 + i)
        sent_x(functools.partial(x_part, q), q)
        sent_g(functools.partial(g_part, q), q)
        place = state_out.at[pl.ds(mult(c * HALF + q * CHUNK, CHUNK), CHUNK), :]
        land = state_out.at[pl.ds(mult(oc * HALF + q * CHUNK, CHUNK), CHUNK), :]
        pltpu.make_async_copy(s_stage.at[c, q], place, f_loc.at[q]).wait()
        remote(s_stage.at[oc, q], land, f_send.at[q], f_recv.at[q], sib).wait()
        for t in range(2):
            remote(s_send.at[t, q], s_recv.at[t, q], st_send.at[t, q], st_recv.at[t, q], after).wait_send()

    for src, dst, i in begin:
        remote(src, dst, m_send.at[i], m_recv.at[i], sib).wait_send()
    for t in range(2):
        remote(tails.at[t + 1, 2], tails.at[t + 1, 0], m_send.at[3 + t], m_recv.at[3 + t], after).wait_send()
    for t in range(3):
        remote(sq_send.at[t], sq_recv.at[t], m_send.at[5 + t], m_recv.at[5 + t], sib).wait_send()

    @pl.loop(0, PIECES)
    def _(n):
        cols = pl.ds(mult(n * PIECE, PIECE), PIECE)
        for t in range(3):
            remote(part_send.at[t, n], part_recv.at[t, n], p_send.at[t, n], p_recv.at[t, n], sib).wait_send()
        for t in range(2):
            part = hid.at[t + 1, c, :, cols]
            remote(pan_send.at[t, :, cols], part, n_send.at[t, n], n_recv.at[t, n], up).wait_send()
            remote(part, part, r_send.at[t, n], r_recv.at[t, n], sib).wait_send()


def local(
    panels, feed, ssm_state, conv_state, w_in, w_out, norm_gain, conv_weight, conv_bias,
    dt_bias, decay_rate, skip_gain, out_gain,
):
    tail = jnp.pad(conv_state[0, 0].astype(F32), ((5, 0), (0, 0)))
    w_dt = jnp.pad(w_in[0, :, 9216:], ((0, 0), (0, 64)))
    heads = jnp.pad(jnp.concatenate([dt_bias, decay_rate], axis=0), ((0, 6), (0, 64)))
    skip = jnp.repeat(skip_gain, 64, axis=1)
    any_ = pl.BlockSpec(memory_space=pl.ANY)
    vmem = pl.BlockSpec(memory_space=pltpu.VMEM)
    dma = pltpu.SemaphoreType.DMA
    scratch = [
        pltpu.VMEM((STEPS, 2048, 512), BF16),
        pltpu.VMEM((2048, 640), BF16),
        pltpu.VMEM((HALF, WIDTH), BF16),
        pltpu.VMEM((3, 2, SEG, WIDTH), BF16),
        pltpu.VMEM((2 * SEG, WIDTH), BF16),
        pltpu.VMEM((2 * SEG, 128), F32),
        pltpu.VMEM((2 * SEG, 128), F32),
        pltpu.VMEM((3, 3, 8, 5120), F32),
        pltpu.VMEM((2, HALF, 128), F32),
        pltpu.VMEM((STEPS, 128, CHUNK), F32),
        pltpu.VMEM((2, STEPS, 128, CHUNK), BF16),
        pltpu.VMEM((2, STEPS, 128, CHUNK), BF16),
        pltpu.VMEM((2, STEPS, CHUNK, 128), F32),
        pltpu.VMEM((2, SEG, WIDTH), BF16),
        pltpu.VMEM((SEG + 8, 256), F32),
        pltpu.VMEM((2 * SEG, 512), F32),
        pltpu.VMEM((2, 2, SEG, 128), BF16),
        pltpu.VMEM((2, 2, SEG, 128), BF16),
        pltpu.VMEM((2, 2, SEG, 128), F32),
        pltpu.VMEM((2, 2, 32, 32), F32),
        pltpu.VMEM((2, SEG, 128), F32),
        pltpu.VMEM((2, 128, 256), F32),
        pltpu.VMEM((2, 128, 256), F32),
        pltpu.VMEM((2, SEG, 128), BF16),
        pltpu.VMEM((2, SEG, 128), BF16),
        pltpu.VMEM((2, 8, 128), F32),
        pltpu.VMEM((2 * SEG, HALF), BF16),
        pltpu.VMEM((PIECES, SEG, PIECE), F32),
        pltpu.VMEM((3, PIECES, SEG, PIECE), BF16),
        pltpu.VMEM((3, PIECES, SEG, PIECE), BF16),
        pltpu.VMEM((2 * SEG, 128), F32),
        pltpu.VMEM((3, SEG, 128), F32),
        pltpu.VMEM((3, SEG, 128), F32),
        pltpu.VMEM((2, SEG, WIDTH), BF16),
        dma((9, 20)), dma((9, 20)), dma((9, 3)), dma((5,)), dma((8,)), dma((8,)),
        dma((3, PIECES)), dma((3, PIECES)), dma((2, PIECES)), dma((2, PIECES)), dma((2, PIECES)), dma((2, PIECES)),
        dma((2, STEPS)), dma((2, STEPS)), dma((STEPS,)), dma((STEPS,)), dma((STEPS,)),
    ]
    panel, state = pl.pallas_call(
        kernel,
        out_shape=(
            jax.ShapeDtypeStruct((SEG, WIDTH), BF16),
            jax.ShapeDtypeStruct((4096, 128), F32),
        ),
        in_specs=[any_, any_, any_, any_, any_, any_, any_] + [vmem] * 6,
        out_specs=(vmem, any_),
        scratch_shapes=scratch,
        compiler_params=pltpu.CompilerParams(
            collective_id=0, has_side_effects=True, vmem_limit_bytes=60 * 1024 * 1024
        ),
        cost_estimate=pl.CostEstimate(flops=28_000_000_000, bytes_accessed=60_000_000, transcendentals=20_000_000),
    )(
        panels[0], feed, ssm_state.reshape(4096, 128), tail, w_in[0], w_dt, w_out[0],
        norm_gain, conv_weight[0], conv_bias, heads, skip, out_gain,
    )
    return (panel[None], state.reshape(1, 1, 64, 64, 128))


def solution(mesh):
    return jax.shard_map(
        local,
        mesh=mesh,
        in_specs=(
            P("layer", "seq", None),
            P(None, "seq", None),
            P("layer", "seq", None, None, None),
            P("layer", "seq", None, None),
            P("layer", "seq", None),
            P("layer", None, None),
            P("layer", None),
            P("layer", None, None),
            P("layer", None),
            P("layer", None),
            P("layer", None),
            P("layer", None),
            P("layer", None),
        ),
        out_specs=(P("layer", "seq", None), P("layer", "seq", None, None, None)),
        check_vma=False,
    )
```

```python
import functools

import jax
import jax.numpy as jnp
from jax import lax
from jax.experimental import pallas as pl
from jax.experimental.pallas import tpu as pltpu
from jax.sharding import PartitionSpec as P

EPS = 1e-05
LOG2E = 1.4426950408889634
F32 = jnp.float32
BF16 = jnp.bfloat16
SEG = 160
WIDTH = 2048
HALF = 2048
CHUNK = 256
STEPS = HALF // CHUNK
PIECE = 512
PIECES = WIDTH // PIECE
MESH = pl.DeviceIdType.MESH
HIGHEST = lax.Precision.HIGHEST


def silu_of_half(half):
    return half + half * jnp.tanh(half)


def dot(a, b):
    return jnp.dot(a, b, preferred_element_type=F32)


def by_rows(v, scale):
    blocks = [v[:, i : i + 128] * scale for i in range(0, v.shape[1], 128)]
    return blocks[0] if len(blocks) == 1 else jnp.concatenate(blocks, axis=1)


def lane_sums(v):
    total = v[:, :128]
    for i in range(128, v.shape[1], 128):
        total = total + v[:, i : i + 128]
    return total


def kernel(
    panels, feed, state_in, w_in, w_out, tail_in, norm_gain, conv_w, conv_b, dt_bias, decay_rate, skip_gain, out_gain,
    panel_out, state_out,
    w_rows, w_cut, bc_cut, heads,
    w_main, w_bc, w_o, hid, hg, ssq, rowscale, tails, s_in, s_loc, s_send, s_recv, s_stage, fd,
    convbuf, proj, spread_out, b_all, c_all, score_a, score_b, ld_col, ld_row, e_all, e_fin,
    gated, own_part, part_send, part_recv, sq_mine, sq_send, sq_recv, pan_send,
    g_send, g_recv, l_sem, m_send, m_recv, p_send, p_recv, n_send, n_recv, r_send, r_recv,
    st_send, st_recv, f_send, f_recv, f_loc,
):
    layer = lax.axis_index("layer")
    seq = lax.axis_index("seq")
    c = lax.rem(seq, 2)
    m = lax.div(seq, 2)
    y = lax.rem(m, 4)
    z = lax.div(m, 4)
    oc = 1 - c
    yp = lax.rem(y + 1, 4)
    ym = lax.rem(y + 3, 4)
    y2 = lax.rem(y + 2, 4)
    oz = 1 - z

    def at(zz, yy, cc):
        return (layer, zz * 8 + yy * 2 + cc)

    sib = at(z, y, oc)
    to_yp = at(z, yp, c)
    to_ym = at(z, ym, c)
    to_z = at(oz, y, c)
    up = (lax.rem(layer + 1, 8), seq)
    down = (lax.rem(layer + 7, 8), seq)
    after = (layer, lax.rem(seq + 2, 16))
    before = (layer, lax.rem(seq + 14, 16))

    def mult(v, by):
        return pl.multiple_of(v, by)

    local = (
        (w_in.at[pl.ds(8192, 1088), :], w_rows.at[pl.ds(8192, 1088), :]),
        (w_in.at[pl.ds(4096, 4096), :], w_rows.at[pl.ds(4096, 4096), :]),
        (w_in.at[pl.ds(0, 4096), :], w_rows.at[pl.ds(0, 4096), :]),
        (panels, hid.at[0, c]),
        (state_in.at[pl.ds(mult(c * HALF, HALF), HALF), :], s_in.at[c]),
        (w_out.at[pl.ds(mult(c * HALF, HALF), HALF), :], w_o),
        (feed, fd),
    )
    for i, (src, dst) in enumerate(local[:3]):
        pltpu.make_async_copy(src, dst, l_sem.at[i]).start()

    barrier = pltpu.get_barrier_semaphore()
    friends = (sib, to_yp, to_ym, to_z, up, down, after, before)
    for friend in friends:
        pl.semaphore_signal(barrier, inc=1, device_id=friend, device_id_type=MESH)

    heads[...] = jnp.zeros((8, 128), F32)
    heads[0:1, 0:64] = dt_bias[...]
    heads[1:2, 0:64] = decay_rate[...]
    heads[2:3, 0:64] = skip_gain[...]
    tails[0, c, 0:8, :] = jnp.zeros((8, 5120), F32)
    tails[0, c, 5:8, :] = tail_in[...].astype(F32)

    for i, (src, dst) in enumerate(local[:3]):
        pltpu.make_async_copy(src, dst, l_sem.at[i]).wait()
    pl.semaphore_wait(barrier, len(friends))

    def remote(src, dst, ss, rs, who):
        return pltpu.make_async_remote_copy(
            src_ref=src, dst_ref=dst, send_sem=ss, recv_sem=rs, device_id=who, device_id_type=MESH
        )

    own_rows = mult(m * 256 + c * 128, 128)
    sib_rows = mult(m * 256 + oc * 128, 128)

    def turned(start, size):
        return w_rows[pl.ds(mult(start, 64), size), :].T

    def bc_prepare():
        dt = jnp.concatenate([turned(9216, 64), jnp.zeros((128, 64), BF16)], axis=1)
        rows = pl.ds(own_rows, 128)
        for cc, target, where in ((c, w_bc, rows), (oc, bc_cut, slice(0, 128))):
            target[where, 0:256] = turned(8192 + cc * 256, 256)
            target[where, 256:512] = turned(8704 + cc * 256, 256)
            target[where, 512:640] = dt
        remote(bc_cut, w_bc.at[rows, :], g_send.at[8, 18], g_recv.at[8, 18], sib).start()

    def main_prepare(q):
        rows = pl.ds(own_rows, 128)
        w_main[q, rows, 0:256] = turned(4096 + c * 2048 + q * 256, 256)
        w_main[q, rows, 256:512] = turned(c * 2048 + q * 256, 256)
        w_cut[q, :, 0:256] = turned(4096 + oc * 2048 + q * 256, 256)
        w_cut[q, :, 256:512] = turned(oc * 2048 + q * 256, 256)
        remote(w_cut.at[q], w_main.at[q, rows, :], g_send.at[q, 18], g_recv.at[q, 18], sib).start()

    def bc_landed():
        return w_bc.at[pl.ds(sib_rows, 128), :]

    def main_landed(q):
        return w_main.at[q, pl.ds(sib_rows, 128), :]

    def bc_part(mm, half=None):
        if half is None:
            return w_bc.at[pl.ds(mult(mm * 256, 256), 256), :]
        return w_bc.at[pl.ds(mult(mm * 256 + half * 128, 128), 128), :]

    def x_part(q, mm, half=None):
        if half is None:
            return w_main.at[q, pl.ds(mult(mm * 256, 256), 256), pl.ds(0, 256)]
        return w_main.at[q, pl.ds(mult(mm * 256 + half * 128, 128), 128), pl.ds(0, 256)]

    def g_part(q, mm, half=None):
        if half is None:
            return w_main.at[q, pl.ds(mult(mm * 256, 256), 256), pl.ds(256, 256)]
        return w_main.at[q, pl.ds(mult(mm * 256 + half * 128, 128), 128), pl.ds(256, 256)]

    m_yp, m_ym, m_y2 = z * 4 + yp, z * 4 + ym, z * 4 + y2
    o_y, o_yp, o_ym, o_y2 = oz * 4 + y, oz * 4 + yp, oz * 4 + ym, oz * 4 + y2

    def push(part, q, slot, who):
        remote(part, part, g_send.at[q, slot], g_recv.at[q, slot], who).start()

    def arrived(part, q, slot):
        remote(part, part, g_send.at[q, slot], g_recv.at[q, slot], sib).wait_recv()

    def sent(part, q, slot):
        remote(part, part, g_send.at[q, slot], g_recv.at[q, slot], sib).wait_send()

    def first_x(part, q):
        push(part(m), q, 2, to_z)
        push(part(m), q, 0, to_yp)
        push(part(m), q, 1, to_ym)

    def first_g(part, q):
        push(part(m), q, 5, to_z)
        push(part(m), q, 3, to_yp)
        push(part(m), q, 4, to_ym)

    def second_x(part, q):
        arrived(part(o_y), q, 2)
        push(part(o_y), q, 6, to_yp)
        push(part(o_y), q, 7, to_ym)
        arrived(part(m_ym), q, 0)
        push(part(m_ym, 0), q, 8, to_yp)
        arrived(part(m_yp), q, 1)
        push(part(m_yp, 1), q, 9, to_ym)

    def second_g(part, q):
        arrived(part(m_ym), q, 3)
        push(part(m_ym), q, 11, to_z)
        push(part(m_ym, 0), q, 10, to_yp)
        arrived(part(m_yp), q, 4)
        push(part(m_yp), q, 13, to_z)
        push(part(m_yp, 1), q, 12, to_ym)
        arrived(part(o_y), q, 5)

    def third_x(part, q):
        arrived(part(o_ym), q, 6)
        push(part(o_ym, 0), q, 14, to_yp)
        arrived(part(o_yp), q, 7)
        push(part(o_yp, 1), q, 15, to_ym)
        arrived(part(m_y2, 0), q, 8)
        arrived(part(m_y2, 1), q, 9)

    def third_g(part, q):
        arrived(part(m_y2, 0), q, 10)
        push(part(m_y2, 0), q, 16, to_z)
        arrived(part(m_y2, 1), q, 12)
        push(part(m_y2, 1), q, 17, to_z)
        arrived(part(o_ym), q, 11)
        arrived(part(o_yp), q, 13)

    def last_x(part, q):
        arrived(part(o_y2, 0), q, 14)
        arrived(part(o_y2, 1), q, 15)

    def last_g(part, q):
        arrived(part(o_y2, 0), q, 16)
        arrived(part(o_y2, 1), q, 17)

    def sent_x(part, q):
        for slot in (0, 1, 2, 6, 7):
            sent(part(m), q, slot)
        for slot in (8, 9, 14, 15):
            sent(part(m, 0), q, slot)

    def sent_g(part, q):
        for slot in (3, 4, 5, 11, 13):
            sent(part(m), q, slot)
        for slot in (10, 12, 16, 17):
            sent(part(m, 0), q, slot)

    bc_prepare()
    main_prepare(0)
    arrived(bc_landed(), 8, 18)
    first_x(bc_part, 8)

    @pl.loop(0, STEPS)
    def _(q):
        @pl.when(q < STEPS - 1)
        def _():
            main_prepare(q + 1)

        arrived(main_landed(q), q, 18)
        first_x(functools.partial(x_part, q), q)
        first_g(functools.partial(g_part, q), q)

    begin = (
        (panels, hid.at[0, c], 0),
        (tails.at[0, c], tails.at[0, c], 1),
        (state_in.at[pl.ds(mult(oc * HALF, HALF), HALF), :], s_in.at[c], 2),
    )
    for src, dst, i in begin:
        remote(src, dst, m_send.at[i], m_recv.at[i], sib).start()
    for i, (src, dst) in enumerate(local[3:]):
        pltpu.make_async_copy(src, dst, l_sem.at[3 + i]).start()
    for i, (src, dst) in enumerate(local[3:]):
        pltpu.make_async_copy(src, dst, l_sem.at[3 + i]).wait()
    for (src, dst, i), land in zip(begin, (hid.at[0, oc], tails.at[0, oc], s_in.at[oc])):
        remote(land, land, m_send.at[i], m_recv.at[i], sib).wait_recv()

    def ingest(t, tile, n):
        cols = pl.ds(mult(n * PIECE, PIECE), PIECE)
        rows = pl.ds(mult(tile * SEG, 32), SEG)
        h = hid[t, tile, :, cols].astype(F32)
        ssq[rows, :] += lane_sums(h * h)
        hg[rows, cols] = (h * norm_gain[:, cols]).astype(BF16)

    lane = lax.broadcasted_iota(jnp.int32, (SEG, 128), 1)
    row = lax.broadcasted_iota(jnp.int32, (SEG, 128), 0)

    def conv(slot, tile_tail, fresh, weight, bias):
        convbuf[slot, 0:8, :] = tile_tail
        convbuf[slot, 8 : 8 + SEG, :] = fresh
        total = bias
        for k in range(4):
            total = total + convbuf[slot, 5 + k : 5 + k + SEG, :] * weight[k : k + 1, :]
        return silu_of_half(total).astype(BF16)

    def tail_of(t, tile, cols):
        value = tails[t, tile, :, cols]
        if t > 0 and tile == 0:
            value = jnp.where(m > 0, value, 0.0)
        return value

    def keep_tail(t, tile, cols, slot):
        if t < 2:
            tails[t + 1, 1 if tile == 0 else 2, :, cols] = convbuf[slot, SEG : SEG + 8, :]

    def prologue(t):
        total = jnp.sum(ssq[...], axis=1, keepdims=True)
        rowscale[...] = jnp.broadcast_to(lax.rsqrt(total * (1.0 / WIDTH) + EPS), (2 * SEG, 128))
        proj[...] = dot(hg[...], w_bc[:, 0:512])
        logits = dot(hg[...], w_bc[:, 512:640])
        causal = lane <= row
        tri = (
            lax.broadcasted_iota(jnp.int32, (SEG, SEG), 1) <= lax.broadcasted_iota(jnp.int32, (SEG, SEG), 0)
        ).astype(F32)
        for tile in range(2):
            rows = slice(tile * SEG, (tile + 1) * SEG)
            scale = rowscale[rows, :]
            for block in range(4):
                slot = block % 2
                base = 4096 if block < 2 else 4608
                cols = pl.ds(mult(base + c * 256 + slot * 128, 128), 128)
                fresh = proj[rows, block * 128 : block * 128 + 128] * scale
                made = conv(tile * 2 + slot, tail_of(t, tile, cols), fresh, 0.5 * conv_w[:, cols], 0.5 * conv_b[:, cols])
                keep_tail(t, tile, cols, tile * 2 + slot)
                target = b_all if block < 2 else c_all
                target[tile, slot] = made
            for g in range(2):
                scores = lax.dot_general(
                    c_all[tile, g], b_all[tile, g], (((1,), (1,)), ((), ())), preferred_element_type=F32
                )
                score_a[tile, g] = jnp.where(causal, scores[:, 0:128], 0.0)
                score_b[tile, g] = jnp.where(causal[0:32, 0:32], scores[128:SEG, 128:SEG], 0.0)
            v = logits[rows, :] * scale + heads[0:1, :]
            step = jnp.maximum(v, 0.0) + jnp.log1p(jnp.exp(-jnp.abs(v)))
            ld = jnp.dot(tri, -heads[1:2, :] * step, preferred_element_type=F32, precision=HIGHEST)
            last = ld[SEG - 1 : SEG, :]
            ld_col[tile] = ld * LOG2E
            ld_row[tile, :, 0:SEG] = (ld * LOG2E - jnp.log2(step)).T
            e_all[2 * tile * SEG : (2 * tile + 1) * SEG, :] = jnp.exp(ld).astype(BF16)
            e_all[(2 * tile + 1) * SEG : (2 * tile + 2) * SEG, :] = (jnp.exp(last - ld) * step).astype(BF16)
            e_fin[tile, 0:1, :] = jnp.exp(last)
            e_fin[tile, 1:2, :] = heads[2:3, :]

    low = lane < 64

    def step_of(t, q):
        g = lax.div(q, 4)
        base = c * 32 + q * 4
        first = lax.rem(128 - base, 128)
        proj[...] = dot(hg[...], w_main[q])
        spread = (
            lax.broadcasted_iota(jnp.int32, (128, CHUNK), 0)
            == base + lax.div(lax.broadcasted_iota(jnp.int32, (128, CHUNK), 1), 64)
        ).astype(F32)
        spread_out[...] = dot(e_all[...], spread.astype(BF16))
        if t > 0:
            remote(s_recv.at[t - 1, q], s_recv.at[t - 1, q], st_send.at[t - 1, q], st_recv.at[t - 1, q], after).wait_recv()
        made = []
        for tile in range(2):
            rows = slice(tile * SEG, (tile + 1) * SEG)
            scale = rowscale[rows, :]
            half_scale = 0.5 * scale
            if t == 0:
                state = s_in[tile, pl.ds(mult(q * CHUNK, CHUNK), CHUNK), :].T
            elif tile == 0:
                state = jnp.where(m > 0, s_recv[t - 1, q].astype(F32), 0.0)
            else:
                state = s_loc[q]
            ld = pltpu.roll(ld_col[tile], first, 1)
            ends = pltpu.roll(e_fin[tile], first, 1)
            sa, sb = score_a[tile, g], score_b[tile, g]
            carried = dot(c_all[tile, g], state.astype(BF16))
            squares = jnp.zeros((SEG, 128), F32)
            grown = []
            for pair in range(2):
                lanes = slice(pair * 128, pair * 128 + 128)
                cols = pl.ds(mult(c * HALF + q * CHUNK + pair * 128, 128), 128)
                slot = tile * 2 + pair
                x = conv(
                    slot, tail_of(t, tile, cols), proj[rows, lanes] * scale, 0.5 * conv_w[:, cols], 0.5 * conv_b[:, cols]
                )
                keep_tail(t, tile, cols, slot)
                weights = []
                for h in (pair * 2, pair * 2 + 1):
                    col = jnp.broadcast_to(ld[:, h : h + 1], (SEG, 128))
                    ldr = ld_row[tile, pl.ds(base + h, 1), :]
                    wa = (sa * jnp.exp2(jnp.minimum(col - ldr[:, 0:128], 64.0))).astype(BF16)
                    wb = (sb * jnp.exp2(jnp.minimum(col[128:SEG, 0:32] - ldr[:, 128:SEG], 64.0))).astype(BF16)
                    wb = jnp.concatenate([jnp.zeros((128, 32), BF16), wb], axis=0)
                    weights.append(jnp.concatenate([wa, wb], axis=1))
                both = dot(jnp.concatenate(weights, axis=0), x)
                mixed = jnp.where(low, both[0:SEG], both[SEG : 2 * SEG])
                wide = x.astype(F32)
                end = jnp.where(low[0:8], ends[:, 2 * pair : 2 * pair + 1], ends[:, 2 * pair + 1 : 2 * pair + 2])
                e_now = spread_out[2 * tile * SEG : (2 * tile + 1) * SEG, lanes]
                e_last = spread_out[(2 * tile + 1) * SEG : (2 * tile + 2) * SEG, lanes]
                combined = mixed + carried[:, lanes] * e_now + end[1:2, :] * wide
                gate = slice(CHUNK + pair * 128, CHUNK + pair * 128 + 128)
                out = combined * silu_of_half(proj[rows, gate] * half_scale)
                squares = squares + out * out
                gated[rows, pl.ds(mult(q * CHUNK + pair * 128, 128), 128)] = (out * out_gain[:, cols]).astype(BF16)
                grew = lax.dot_general(
                    b_all[tile, g], (wide * e_last).astype(BF16), (((0,), (0,)), ((), ())), preferred_element_type=F32
                )
                grown.append(end[0:1, :] * state[:, lanes] + grew)
            sq_mine[rows, :] += squares
            made.append(jnp.concatenate(grown, axis=1))
        if t < 2:
            s_loc[q] = made[0]
            s_send[t, q] = made[1].astype(BF16)
            remote(s_send.at[t, q], s_recv.at[t, q], st_send.at[t, q], st_recv.at[t, q], after).start()
        else:
            s_stage[0, q] = made[0].T
            s_stage[1, q] = made[1].T
            place = state_out.at[pl.ds(mult(c * HALF + q * CHUNK, CHUNK), CHUNK), :]
            pltpu.make_async_copy(s_stage.at[c, q], place, f_loc.at[q]).start()
            remote(s_stage.at[oc, q], place, f_send.at[q], f_recv.at[q], sib).start()

    own = pl.ds(mult(c * SEG, 32), SEG)
    other = pl.ds(mult(oc * SEG, 32), SEG)

    def project_out(t, n):
        cols = pl.ds(mult(n * PIECE, PIECE), PIECE)
        proj[...] = dot(gated[...], w_o[:, cols])
        part_send[t, n] = proj[other, :].astype(BF16)
        own_part[n] = proj[own, :]
        remote(part_send.at[t, n], part_recv.at[t, n], p_send.at[t, n], p_recv.at[t, n], sib).start()

    def finish(t, n, scale):
        cols = pl.ds(mult(n * PIECE, PIECE), PIECE)
        remote(part_recv.at[t, n], part_recv.at[t, n], p_send.at[t, n], p_recv.at[t, n], sib).wait_recv()
        whole = own_part[n] + part_recv[t, n].astype(F32)
        panel = (hid[t, c, :, cols].astype(F32) + by_rows(whole, scale)).astype(BF16)
        if t < 2:
            pan_send[t, :, cols] = jnp.where(layer == 7, fd[t, :, cols].astype(F32), panel.astype(F32)).astype(BF16)
            remote(
                pan_send.at[t, :, cols], hid.at[t + 1, c, :, cols], n_send.at[t, n], n_recv.at[t, n], up
            ).start()
        else:
            panel_out[:, cols] = panel

    for t in range(3):
        ssq[...] = jnp.zeros((2 * SEG, 128), F32)
        sq_mine[...] = jnp.zeros((2 * SEG, 128), F32)
        if t == 0:

            @pl.loop(0, 2 * PIECES)
            def _(i):
                ingest(0, lax.rem(i, 2), lax.div(i, 2))

            second_x(bc_part, 8)

            @pl.loop(0, STEPS)
            def _(q):
                second_x(functools.partial(x_part, q), q)
                second_g(functools.partial(g_part, q), q)

            third_x(bc_part, 8)

            @pl.loop(0, STEPS)
            def _(q):
                third_x(functools.partial(x_part, q), q)
                third_g(functools.partial(g_part, q), q)

            last_x(bc_part, 8)
        else:

            @pl.loop(0, PIECES)
            def _(n):
                part = hid.at[t, c, :, pl.ds(mult(n * PIECE, PIECE), PIECE)]
                remote(part, part, n_send.at[t - 1, n], n_recv.at[t - 1, n], up).wait_recv()
                remote(part, part, r_send.at[t - 1, n], r_recv.at[t - 1, n], sib).start()
                ingest(t, c, n)

            @pl.loop(0, PIECES)
            def _(n):
                part = hid.at[t, oc, :, pl.ds(mult(n * PIECE, PIECE), PIECE)]
                remote(part, part, r_send.at[t - 1, n], r_recv.at[t - 1, n], sib).wait_recv()
                ingest(t, oc, n)

            remote(tails.at[t, 0], tails.at[t, 0], m_send.at[2 + t], m_recv.at[2 + t], after).wait_recv()
        prologue(t)

        @pl.loop(0, STEPS)
        def _(q):
            if t == 0:
                last_x(functools.partial(x_part, q), q)
                last_g(functools.partial(g_part, q), q)
            step_of(t, q)

        if t < 2:
            remote(tails.at[t + 1, 2], tails.at[t + 1, 0], m_send.at[3 + t], m_recv.at[3 + t], after).start()
        sq_send[t] = sq_mine[other, :]
        remote(sq_send.at[t], sq_recv.at[t], m_send.at[5 + t], m_recv.at[5 + t], sib).start()
        project_out(t, 0)
        remote(sq_recv.at[t], sq_recv.at[t], m_send.at[5 + t], m_recv.at[5 + t], sib).wait_recv()
        squares = jnp.sum(sq_mine[own, :] + sq_recv[t], axis=1, keepdims=True)
        rowscale[0:SEG, :] = jnp.broadcast_to(lax.rsqrt(squares * (1.0 / 4096) + EPS), (SEG, 128))

        @pl.loop(1, PIECES)
        def _(n):
            project_out(t, n)
            finish(t, n - 1, rowscale[0:SEG, :])

        finish(t, PIECES - 1, rowscale[0:SEG, :])

    sent(bc_landed(), 8, 18)
    sent_x(bc_part, 8)

    @pl.loop(0, STEPS)
    def _(q):
        sent(main_landed(q), q, 18)
        sent_x(functools.partial(x_part, q), q)
        sent_g(functools.partial(g_part, q), q)
        place = state_out.at[pl.ds(mult(c * HALF + q * CHUNK, CHUNK), CHUNK), :]
        land = state_out.at[pl.ds(mult(oc * HALF + q * CHUNK, CHUNK), CHUNK), :]
        pltpu.make_async_copy(s_stage.at[c, q], place, f_loc.at[q]).wait()
        remote(s_stage.at[oc, q], land, f_send.at[q], f_recv.at[q], sib).wait()
        for t in range(2):
            remote(s_send.at[t, q], s_recv.at[t, q], st_send.at[t, q], st_recv.at[t, q], after).wait_send()

    for src, dst, i in begin:
        remote(src, dst, m_send.at[i], m_recv.at[i], sib).wait_send()
    for t in range(2):
        remote(tails.at[t + 1, 2], tails.at[t + 1, 0], m_send.at[3 + t], m_recv.at[3 + t], after).wait_send()
    for t in range(3):
        remote(sq_send.at[t], sq_recv.at[t], m_send.at[5 + t], m_recv.at[5 + t], sib).wait_send()

    @pl.loop(0, PIECES)
    def _(n):
        cols = pl.ds(mult(n * PIECE, PIECE), PIECE)
        for t in range(3):
            remote(part_send.at[t, n], part_recv.at[t, n], p_send.at[t, n], p_recv.at[t, n], sib).wait_send()
        for t in range(2):
            part = hid.at[t + 1, c, :, cols]
            remote(pan_send.at[t, :, cols], part, n_send.at[t, n], n_recv.at[t, n], up).wait_send()
            remote(part, part, r_send.at[t, n], r_recv.at[t, n], sib).wait_send()


def hand_over(panel, state, panel_out, state_out, panel_here, state_here, sem_in, sem_out):
    pieces = [(panel, panel_here, panel_out)]
    for i in range(4):
        rows = pl.ds(i * 1024, 1024)
        pieces.append((state.at[rows, :], state_here.at[rows, :], state_out.at[rows, :]))
    for i, (src, here, _) in enumerate(pieces):
        pltpu.make_async_copy(src, here, sem_in.at[i]).start()
    for i, (src, here, dst) in enumerate(pieces):
        pltpu.make_async_copy(src, here, sem_in.at[i]).wait()
        pltpu.make_async_copy(here, dst, sem_out.at[i]).start()
    for i, (_, here, dst) in enumerate(pieces):
        pltpu.make_async_copy(here, dst, sem_out.at[i]).wait()


def local(
    panels, feed, ssm_state, conv_state, w_in, w_out, norm_gain, conv_weight, conv_bias,
    dt_bias, decay_rate, skip_gain, out_gain,
):
    any_ = pl.BlockSpec(memory_space=pl.ANY)
    vmem = pl.BlockSpec(memory_space=pltpu.VMEM)
    dma = pltpu.SemaphoreType.DMA
    scratch = [
        pltpu.VMEM((9280, 128), BF16),
        pltpu.VMEM((STEPS, 128, 512), BF16),
        pltpu.VMEM((128, 640), BF16),
        pltpu.VMEM((8, 128), F32),
        pltpu.VMEM((STEPS, 2048, 512), BF16),
        pltpu.VMEM((2048, 640), BF16),
        pltpu.VMEM((HALF, WIDTH), BF16),
        pltpu.VMEM((3, 2, SEG, WIDTH), BF16),
        pltpu.VMEM((2 * SEG, WIDTH), BF16),
        pltpu.VMEM((2 * SEG, 128), F32),
        pltpu.VMEM((2 * SEG, 128), F32),
        pltpu.VMEM((3, 3, 8, 5120), F32),
        pltpu.VMEM((2, HALF, 128), F32),
        pltpu.VMEM((STEPS, 128, CHUNK), F32),
        pltpu.VMEM((2, STEPS, 128, CHUNK), BF16),
        pltpu.VMEM((2, STEPS, 128, CHUNK), BF16),
        pltpu.VMEM((2, STEPS, CHUNK, 128), F32),
        pltpu.VMEM((2, SEG, WIDTH), BF16),
        pltpu.VMEM((4, SEG + 8, 128), F32),
        pltpu.VMEM((2 * SEG, 512), F32),
        pltpu.VMEM((4 * SEG, CHUNK), F32),
        pltpu.VMEM((2, 2, SEG, 128), BF16),
        pltpu.VMEM((2, 2, SEG, 128), BF16),
        pltpu.VMEM((2, 2, SEG, 128), F32),
        pltpu.VMEM((2, 2, 32, 32), F32),
        pltpu.VMEM((2, SEG, 128), F32),
        pltpu.VMEM((2, 128, 256), F32),
        pltpu.VMEM((4 * SEG, 128), BF16),
        pltpu.VMEM((2, 8, 128), F32),
        pltpu.VMEM((2 * SEG, HALF), BF16),
        pltpu.VMEM((PIECES, SEG, PIECE), F32),
        pltpu.VMEM((3, PIECES, SEG, PIECE), BF16),
        pltpu.VMEM((3, PIECES, SEG, PIECE), BF16),
        pltpu.VMEM((2 * SEG, 128), F32),
        pltpu.VMEM((3, SEG, 128), F32),
        pltpu.VMEM((3, SEG, 128), F32),
        pltpu.VMEM((2, SEG, WIDTH), BF16),
        dma((9, 19)), dma((9, 19)), dma((7,)), dma((8,)), dma((8,)),
        dma((3, PIECES)), dma((3, PIECES)), dma((2, PIECES)), dma((2, PIECES)), dma((2, PIECES)), dma((2, PIECES)),
        dma((2, STEPS)), dma((2, STEPS)), dma((STEPS,)), dma((STEPS,)), dma((STEPS,)),
    ]
    panel, state = pl.pallas_call(
        kernel,
        out_shape=(
            jax.ShapeDtypeStruct((SEG, WIDTH), BF16),
            jax.ShapeDtypeStruct((4096, 128), F32),
        ),
        in_specs=[any_] * 5 + [vmem] * 8,
        out_specs=(vmem, any_),
        scratch_shapes=scratch,
        compiler_params=pltpu.CompilerParams(
            collective_id=0, has_side_effects=True, vmem_limit_bytes=60 * 1024 * 1024
        ),
        cost_estimate=pl.CostEstimate(flops=28_000_000_000, bytes_accessed=60_000_000, transcendentals=20_000_000),
    )(
        panels[0], feed, ssm_state.reshape(4096, 128), w_in[0].T, w_out[0], conv_state[0, 0],
        norm_gain, conv_weight[0], conv_bias, dt_bias, decay_rate, skip_gain, out_gain,
    )
    panel, state = pl.pallas_call(
        hand_over,
        out_shape=(jax.ShapeDtypeStruct((SEG, WIDTH), BF16), jax.ShapeDtypeStruct((4096, 128), F32)),
        in_specs=[any_, any_],
        out_specs=(any_, any_),
        scratch_shapes=[pltpu.VMEM((SEG, WIDTH), BF16), pltpu.VMEM((4096, 128), F32), dma((5,)), dma((5,))],
        compiler_params=pltpu.CompilerParams(vmem_limit_bytes=60 * 1024 * 1024),
    )(panel, state)
    return (panel[None], state.reshape(1, 1, 64, 64, 128))


def solution(mesh):
    return jax.shard_map(
        local,
        mesh=mesh,
        in_specs=(
            P("layer", "seq", None),
            P(None, "seq", None),
            P("layer", "seq", None, None, None),
            P("layer", "seq", None, None),
            P("layer", "seq", None),
            P("layer", None, None),
            P("layer", None),
            P("layer", None, None),
            P("layer", None),
            P("layer", None),
            P("layer", None),
            P("layer", None),
            P("layer", None),
        ),
        out_specs=(P("layer", "seq", None), P("layer", "seq", None, None, None)),
        check_vma=False,
    )
```

```python
import functools

import jax
import jax.numpy as jnp
from jax import lax
from jax.experimental import pallas as pl
from jax.experimental.pallas import tpu as pltpu
from jax.sharding import PartitionSpec as P

EPS = 1e-05
LOG2E = 1.4426950408889634
F32 = jnp.float32
BF16 = jnp.bfloat16
SEG = 160
WIDTH = 2048
HALF = 2048
CHUNK = 256
STEPS = HALF // CHUNK
PIECE = 512
PIECES = WIDTH // PIECE
MESH = pl.DeviceIdType.MESH


def silu_of_half(half):
    return half + half * jnp.tanh(half)


def dot(a, b):
    return jnp.dot(a, b, preferred_element_type=F32)


def by_rows(v, scale):
    blocks = [v[:, i : i + 128] * scale for i in range(0, v.shape[1], 128)]
    return blocks[0] if len(blocks) == 1 else jnp.concatenate(blocks, axis=1)


def lane_sums(v):
    total = v[:, :128]
    for i in range(128, v.shape[1], 128):
        total = total + v[:, i : i + 128]
    return total


def kernel(
    panels, feed, state_in, w_in, w_out, tail_in, norm_gain, conv_w, conv_b, dt_bias, decay_rate, skip_gain, out_gain,
    panel_out, state_out,
    w_rows, w_cut, bc_cut, heads,
    w_main, w_bc, w_o, hid, hg, ssq, rowscale, tails, x_loc, bc_loc, bc_to, bc_from, s_in, s_loc, s_send, s_recv, fd,
    convbuf, proj, made_a, made_b, b_all, c_all, score_a, score_b, ld_col, ld_row, e_all, e_fin,
    gated, own_part, part_send, part_recv, sq_mine, sq_send, sq_recv, pan_send, pan_stage,
    g_send, g_recv, l_sem, m_send, m_recv, p_send, p_recv, n_send, n_recv, r_send, r_recv,
    st_send, st_recv, f_send, f_recv, f_loc, q_send, q_recv, o_send, o_recv, o_loc,
):
    layer = lax.axis_index("layer")
    seq = lax.axis_index("seq")
    c = lax.rem(seq, 2)
    m = lax.div(seq, 2)
    y = lax.rem(m, 4)
    z = lax.div(m, 4)
    oc = 1 - c
    yp = lax.rem(y + 1, 4)
    ym = lax.rem(y + 3, 4)
    y2 = lax.rem(y + 2, 4)
    oz = 1 - z

    def at(zz, yy, cc):
        return (layer, zz * 8 + yy * 2 + cc)

    sib = at(z, y, oc)
    to_yp = at(z, yp, c)
    to_ym = at(z, ym, c)
    to_z = at(oz, y, c)
    up = (lax.rem(layer + 1, 8), seq)
    down = (lax.rem(layer + 7, 8), seq)
    after = (layer, lax.rem(seq + 2, 16))
    before = (layer, lax.rem(seq + 14, 16))

    def mult(v, by):
        return pl.multiple_of(v, by)

    local = (
        (w_in.at[pl.ds(8192, 1088), :], w_rows.at[pl.ds(8192, 1088), :]),
        (w_in.at[pl.ds(4096, 4096), :], w_rows.at[pl.ds(4096, 4096), :]),
        (w_in.at[pl.ds(0, 4096), :], w_rows.at[pl.ds(0, 4096), :]),
        (panels, hid.at[0, c]),
        (state_in.at[pl.ds(mult(c * HALF, HALF), HALF), :], s_in.at[c]),
        (w_out.at[pl.ds(mult(c * HALF, HALF), HALF), :], w_o),
        (feed.at[:, :, pl.ds(mult(c * 1024, 1024), 1024)], fd.at[:, c]),
    )
    for i, (src, dst) in enumerate(local[:3]):
        pltpu.make_async_copy(src, dst, l_sem.at[i]).start()

    barrier = pltpu.get_barrier_semaphore()
    friends = (sib, to_yp, to_ym, to_z, up, down, after, before)
    for friend in friends:
        pl.semaphore_signal(barrier, inc=1, device_id=friend, device_id_type=MESH)

    heads[...] = jnp.zeros((8, 128), F32)
    heads[0:1, 0:64] = dt_bias[...]
    heads[1:2, 0:64] = decay_rate[...]
    heads[2:3, 0:64] = skip_gain[...]
    tails[c, 0:8, :] = jnp.zeros((8, 5120), F32)
    tails[c, 5:8, :] = tail_in[...].astype(F32)

    for i, (src, dst) in enumerate(local[:3]):
        pltpu.make_async_copy(src, dst, l_sem.at[i]).wait()
    pl.semaphore_wait(barrier, len(friends))

    def remote(src, dst, ss, rs, who):
        return pltpu.make_async_remote_copy(
            src_ref=src, dst_ref=dst, send_sem=ss, recv_sem=rs, device_id=who, device_id_type=MESH
        )

    own_rows = mult(m * 256 + c * 128, 128)
    sib_rows = mult(m * 256 + oc * 128, 128)

    def turned(start, size):
        return w_rows[pl.ds(mult(start, 64), size), :].T

    def bc_prepare():
        dt = jnp.concatenate([turned(9216, 64), jnp.zeros((128, 64), BF16)], axis=1)
        rows = pl.ds(own_rows, 128)
        for cc, target, where in ((c, w_bc, rows), (oc, bc_cut, slice(0, 128))):
            target[where, 0:256] = turned(8192 + cc * 256, 256)
            target[where, 256:512] = turned(8704 + cc * 256, 256)
            target[where, 512:640] = dt
        remote(bc_cut, w_bc.at[rows, :], g_send.at[8, 18], g_recv.at[8, 18], sib).start()

    def main_prepare(q):
        rows = pl.ds(own_rows, 128)
        w_main[q, rows, 0:256] = turned(4096 + c * 2048 + q * 256, 256)
        w_main[q, rows, 256:512] = turned(c * 2048 + q * 256, 256)
        w_cut[q, :, 0:256] = turned(4096 + oc * 2048 + q * 256, 256)
        w_cut[q, :, 256:512] = turned(oc * 2048 + q * 256, 256)
        remote(w_cut.at[q], w_main.at[q, rows, :], g_send.at[q, 18], g_recv.at[q, 18], sib).start()

    def bc_landed():
        return w_bc.at[pl.ds(sib_rows, 128), :]

    def main_landed(q):
        return w_main.at[q, pl.ds(sib_rows, 128), :]

    def bc_part(mm, half=None):
        if half is None:
            return w_bc.at[pl.ds(mult(mm * 256, 256), 256), :]
        return w_bc.at[pl.ds(mult(mm * 256 + half * 128, 128), 128), :]

    def main_part(q, mm, half=None):
        if half is None:
            return w_main.at[q, pl.ds(mult(mm * 256, 256), 256), :]
        return w_main.at[q, pl.ds(mult(mm * 256 + half * 128, 128), 128), :]

    def part_of(q):
        return functools.partial(main_part, q)

    m_yp, m_ym, m_y2 = z * 4 + yp, z * 4 + ym, z * 4 + y2
    o_y, o_yp, o_ym, o_y2 = oz * 4 + y, oz * 4 + yp, oz * 4 + ym, oz * 4 + y2

    def push(part, q, slot, who):
        remote(part, part, g_send.at[q, slot], g_recv.at[q, slot], who).start()

    def arrived(part, q, slot):
        remote(part, part, g_send.at[q, slot], g_recv.at[q, slot], sib).wait_recv()

    def sent(part, q, slot):
        remote(part, part, g_send.at[q, slot], g_recv.at[q, slot], sib).wait_send()

    def first_x(part, q):
        push(part(m), q, 2, to_z)
        push(part(m), q, 0, to_yp)
        push(part(m), q, 1, to_ym)

    def first_g(part, q):
        push(part(m), q, 5, to_z)
        push(part(m), q, 3, to_yp)
        push(part(m), q, 4, to_ym)

    def second_x(part, q):
        arrived(part(o_y), q, 2)
        push(part(o_y), q, 6, to_yp)
        push(part(o_y), q, 7, to_ym)
        arrived(part(m_ym), q, 0)
        push(part(m_ym, 0), q, 8, to_yp)
        arrived(part(m_yp), q, 1)
        push(part(m_yp, 1), q, 9, to_ym)

    def second_g(part, q):
        arrived(part(m_ym), q, 3)
        push(part(m_ym), q, 11, to_z)
        push(part(m_ym, 0), q, 10, to_yp)
        arrived(part(m_yp), q, 4)
        push(part(m_yp), q, 13, to_z)
        push(part(m_yp, 1), q, 12, to_ym)
        arrived(part(o_y), q, 5)

    def third_x(part, q):
        arrived(part(o_ym), q, 6)
        push(part(o_ym, 0), q, 14, to_yp)
        arrived(part(o_yp), q, 7)
        push(part(o_yp, 1), q, 15, to_ym)
        arrived(part(m_y2, 0), q, 8)
        arrived(part(m_y2, 1), q, 9)

    def third_g(part, q):
        arrived(part(m_y2, 0), q, 10)
        push(part(m_y2, 0), q, 16, to_z)
        arrived(part(m_y2, 1), q, 12)
        push(part(m_y2, 1), q, 17, to_z)
        arrived(part(o_ym), q, 11)
        arrived(part(o_yp), q, 13)

    def last_x(part, q):
        arrived(part(o_y2, 0), q, 14)
        arrived(part(o_y2, 1), q, 15)

    def last_g(part, q):
        arrived(part(o_y2, 0), q, 16)
        arrived(part(o_y2, 1), q, 17)

    def sent_x(part, q):
        for slot in (0, 1, 2, 6, 7):
            sent(part(m), q, slot)
        for slot in (8, 9, 14, 15):
            sent(part(m, 0), q, slot)

    def sent_g(part, q):
        for slot in (3, 4, 5, 11, 13):
            sent(part(m), q, slot)
        for slot in (10, 12, 16, 17):
            sent(part(m, 0), q, slot)

    bc_prepare()
    main_prepare(0)
    arrived(bc_landed(), 8, 18)
    first_x(bc_part, 8)

    @pl.loop(0, STEPS // 2)
    def _(i):
        q = 2 * i
        main_prepare(q + 1)
        arrived(main_landed(q), q, 18)
        first_x(part_of(q), q)

        @pl.when(i < STEPS // 2 - 1)
        def _():
            main_prepare(q + 2)

        arrived(main_landed(q + 1), q + 1, 18)
        first_g(part_of(q + 1), q + 1)

    begin = (
        (panels, hid.at[0, c], 0),
        (tails.at[c], tails.at[c], 1),
        (state_in.at[pl.ds(mult(oc * HALF, HALF), HALF), :], s_in.at[c], 2),
        (feed.at[:, :, pl.ds(mult(oc * 1024, 1024), 1024)], fd.at[:, c], 3),
    )
    for src, dst, i in begin:
        remote(src, dst, m_send.at[i], m_recv.at[i], sib).start()
    for i, (src, dst) in enumerate(local[3:]):
        pltpu.make_async_copy(src, dst, l_sem.at[3 + i]).start()
    for i, (src, dst) in enumerate(local[3:]):
        pltpu.make_async_copy(src, dst, l_sem.at[3 + i]).wait()
    for (src, dst, i), land in zip(begin, (hid.at[0, oc], tails.at[oc], s_in.at[oc], fd.at[:, oc])):
        remote(land, land, m_send.at[i], m_recv.at[i], sib).wait_recv()

    def ingest(t, tile, n):
        cols = pl.ds(mult(n * PIECE, PIECE), PIECE)
        rows = pl.ds(mult(tile * SEG, 32), SEG)
        h = hid[t, tile, :, cols].astype(F32)
        ssq[rows, :] += lane_sums(h * h)
        hg[rows, cols] = (h * norm_gain[:, cols]).astype(BF16)

    lane = lax.broadcasted_iota(jnp.int32, (SEG, 128), 1)
    row = lax.broadcasted_iota(jnp.int32, (SEG, 128), 0)

    def conv(slot, tile_tail, fresh, weight, bias):
        convbuf[slot, 0:8, :] = tile_tail
        convbuf[slot, 8 : 8 + SEG, :] = fresh
        total = bias
        for k in range(4):
            total = total + convbuf[slot, 5 + k : 5 + k + SEG, :] * weight[k : k + 1, :]
        return silu_of_half(total).astype(BF16)

    def x_tail(t, tile, q, pair, cols):
        lanes = slice(pair * 128, pair * 128 + 128)
        if t == 0:
            return tails[tile, :, cols]
        if tile == 1:
            return x_loc[t - 1, q, :, lanes]
        return jnp.where(m > 0, s_recv[t - 1, q, 128:144, lanes].astype(F32)[8:16], 0.0)

    def bc_tail(t, tile, block, cols):
        lanes = slice(block * 128, block * 128 + 128)
        if t == 0:
            return tails[tile, :, cols]
        if tile == 1:
            return bc_loc[t - 1, :, lanes]
        return jnp.where(m > 0, bc_from[t - 1, :, lanes].astype(F32)[8:16], 0.0)

    def keep_tail(t, tile, slot, here, away):
        if t < 2 and tile == 0:
            target, at_ = here
            target[at_] = convbuf[slot, SEG : SEG + 8, :]
        elif t < 2:
            target, at_ = away
            target[at_] = convbuf[slot, SEG - 8 : SEG + 8, :].astype(BF16)

    def prologue(t, tile):
        rows = slice(tile * SEG, (tile + 1) * SEG)
        if t > 0 and tile == 0:
            remote(bc_to.at[t - 1], bc_from.at[t - 1], m_send.at[3 + t], m_recv.at[3 + t], after).wait_recv()
        total = jnp.sum(ssq[rows, :], axis=1, keepdims=True)
        rowscale[rows, :] = jnp.broadcast_to(lax.rsqrt(total * (1.0 / WIDTH) + EPS), (SEG, 128))
        proj[...] = dot(hg[rows, :], w_bc[...])
        causal = lane <= row
        tri = (
            lax.broadcasted_iota(jnp.int32, (SEG, SEG), 1) <= lax.broadcasted_iota(jnp.int32, (SEG, SEG), 0)
        ).astype(BF16)
        sq_mine[rows, :] = jnp.zeros((SEG, 128), F32)
        scale = rowscale[rows, :]
        for block in range(4):
            slot = block % 2
            base = 4096 if block < 2 else 4608
            cols = pl.ds(mult(base + c * 256 + slot * 128, 128), 128)
            fresh = proj[:, block * 128 : block * 128 + 128] * scale
            made = conv(
                tile * 2 + slot, bc_tail(t, tile, block, cols), fresh, 0.5 * conv_w[:, cols], 0.5 * conv_b[:, cols]
            )
            lanes = slice(block * 128, block * 128 + 128)
            keep_tail(t, tile, tile * 2 + slot, (bc_loc, (min(t, 1), slice(0, 8), lanes)), (bc_to, (min(t, 1), slice(0, 16), lanes)))
            target = b_all if block < 2 else c_all
            target[tile, slot] = made
        for g in range(2):
            scores = lax.dot_general(
                c_all[tile, g], b_all[tile, g], (((1,), (1,)), ((), ())), preferred_element_type=F32
            )
            score_a[tile, g] = jnp.where(causal, scores[:, 0:128], 0.0)
            score_b[tile, g] = jnp.where(causal[0:32, 0:32], scores[128:SEG, 128:SEG], 0.0)
        v = proj[:, 512:640] * scale + heads[0:1, :]
        step = jnp.maximum(v, 0.0) + jnp.log1p(jnp.exp(-jnp.abs(v)))
        fall = -heads[1:2, :] * step
        coarse = fall.astype(BF16)
        rest = fall - coarse.astype(F32)
        fine = rest.astype(BF16)
        finest = (rest - fine.astype(F32)).astype(BF16)
        sums = dot(tri, jnp.concatenate([coarse, fine, finest], axis=1))
        ld = sums[:, 0:128] + (sums[:, 128:256] + sums[:, 256:384])
        last = ld[SEG - 1 : SEG, :]
        ld_col[tile] = ld * LOG2E
        ld_row[tile, :, 0:SEG] = (ld * LOG2E - jnp.log2(step)).T
        e_all[2 * tile * SEG : (2 * tile + 1) * SEG, :] = jnp.exp(ld).astype(BF16)
        e_all[(2 * tile + 1) * SEG : (2 * tile + 2) * SEG, :] = (jnp.exp(last - ld) * step).astype(BF16)
        e_fin[tile, 0:1, :] = jnp.exp(last)
        e_fin[tile, 1:2, :] = heads[2:3, :]

        if t < 2 and tile == 1:
            remote(bc_to.at[t], bc_from.at[t], m_send.at[4 + t], m_recv.at[4 + t], after).start()

    low = lane < 64

    def project(tile, q, into):
        into[...] = dot(hg[tile * SEG : (tile + 1) * SEG, :], w_main[q])

    def state_arrived(t, q):
        land = s_recv.at[t - 1, q]
        remote(land, land, st_send.at[t - 1, q], st_recv.at[t - 1, q], after).wait_recv()

    def step_of(t, tile, q, made_of):
        rows = slice(tile * SEG, (tile + 1) * SEG)
        g = lax.div(q, 4)
        base = c * 32 + q * 4
        first = lax.rem(128 - base, 128)
        spread = (
            lax.broadcasted_iota(jnp.int32, (128, CHUNK), 0)
            == base + lax.div(lax.broadcasted_iota(jnp.int32, (128, CHUNK), 1), 64)
        ).astype(F32)
        both_e = slice(2 * tile * SEG, (2 * tile + 2) * SEG)
        spread_out = dot(e_all[both_e, :], spread.astype(BF16))
        scale = rowscale[rows, :]
        half_scale = 0.5 * scale
        if t == 0:
            state = s_in[tile, pl.ds(mult(q * CHUNK, CHUNK), CHUNK), :].T
        elif tile == 0:
            state = jnp.where(m > 0, s_recv[t - 1, q, 0:128, :].astype(F32), 0.0)
        else:
            state = s_loc[t - 1, q]
        ld = pltpu.roll(ld_col[tile], first, 1)
        ends = pltpu.roll(e_fin[tile], first, 1)
        sa, sb = score_a[tile, g], score_b[tile, g]
        carried = dot(c_all[tile, g], state.astype(BF16))
        squares = jnp.zeros((SEG, 128), F32)
        grown = []
        for pair in range(2):
            lanes = slice(pair * 128, pair * 128 + 128)
            cols = pl.ds(mult(c * HALF + q * CHUNK + pair * 128, 128), 128)
            slot = tile * 2 + pair
            x = conv(
                slot, x_tail(t, tile, q, pair, cols), made_of[:, lanes] * scale, 0.5 * conv_w[:, cols], 0.5 * conv_b[:, cols]
            )
            keep_tail(t, tile, slot, (x_loc, (min(t, 1), q, slice(0, 8), lanes)), (s_send, (min(t, 1), q, slice(128, 144), lanes)))
            weights = []
            for h in (pair * 2, pair * 2 + 1):
                col = jnp.broadcast_to(ld[:, h : h + 1], (SEG, 128))
                ldr = ld_row[tile, pl.ds(base + h, 1), :]
                wa = (sa * jnp.exp2(jnp.minimum(col - ldr[:, 0:128], 64.0))).astype(BF16)
                wb = (sb * jnp.exp2(jnp.minimum(col[128:SEG, 0:32] - ldr[:, 128:SEG], 64.0))).astype(BF16)
                wb = jnp.concatenate([jnp.zeros((128, 32), BF16), wb], axis=0)
                weights.append(jnp.concatenate([wa, wb], axis=1))
            both = dot(jnp.concatenate(weights, axis=0), x)
            mixed = jnp.where(low, both[0:SEG], both[SEG : 2 * SEG])
            wide = x.astype(F32)
            end = jnp.where(low[0:8], ends[:, 2 * pair : 2 * pair + 1], ends[:, 2 * pair + 1 : 2 * pair + 2])
            e_now = spread_out[0:SEG, lanes]
            e_last = spread_out[SEG : 2 * SEG, lanes]
            combined = mixed + carried[:, lanes] * e_now + end[1:2, :] * wide
            gate = slice(CHUNK + pair * 128, CHUNK + pair * 128 + 128)
            out = combined * silu_of_half(made_of[:, gate] * half_scale)
            squares = squares + out * out
            gated[rows, pl.ds(mult(q * CHUNK + pair * 128, 128), 128)] = (out * out_gain[:, cols]).astype(BF16)
            grew = lax.dot_general(
                b_all[tile, g], (wide * e_last).astype(BF16), (((0,), (0,)), ((), ())), preferred_element_type=F32
            )
            grown.append(end[0:1, :] * state[:, lanes] + grew)
        sq_mine[rows, :] += squares
        made = jnp.concatenate(grown, axis=1)
        if t < 2 and tile == 0:
            s_loc[t, q] = made
        elif t < 2:
            s_send[t, q, 0:128, :] = made.astype(BF16)
        else:
            s_in[tile, pl.ds(mult(q * CHUNK, CHUNK), CHUNK), :] = made.T

    def state_off(t, tile, q):
        if t < 2 and tile == 1:
            remote(s_send.at[t, q], s_recv.at[t, q], st_send.at[t, q], st_recv.at[t, q], after).start()
        elif t == 2:
            place = state_out.at[pl.ds(mult(c * HALF + q * CHUNK, CHUNK), CHUNK), :]
            turned_q = pl.ds(mult(q * CHUNK, CHUNK), CHUNK)

            @pl.when(c == tile)
            def _():
                pltpu.make_async_copy(s_in.at[tile, turned_q, :], place, f_loc.at[q]).start()

            @pl.when(c != tile)
            def _():
                remote(s_in.at[tile, turned_q, :], place, f_send.at[q], f_recv.at[q], sib).start()

    def piece_cols(half, p):
        return pl.ds(mult(half * 1024 + p * PIECE, PIECE), PIECE)

    def emit(t, tile):
        rows = slice(tile * SEG, (tile + 1) * SEG)
        sq_send[t, tile] = sq_mine[rows, :]
        remote(sq_send.at[t, tile], sq_recv.at[t, tile], q_send.at[t, tile], q_recv.at[t, tile], sib).start()

        @pl.loop(0, 2)
        def _(p):
            part_send[t, tile, p] = dot(gated[rows, :], w_o[:, piece_cols(oc, p)]).astype(BF16)
            remote(
                part_send.at[t, tile, p], part_recv.at[t, tile, p], p_send.at[t, tile, p], p_recv.at[t, tile, p], sib
            ).start()

        @pl.loop(0, 2)
        def _(p):
            own_part[p] = dot(gated[rows, :], w_o[:, piece_cols(c, p)])

        if (t, tile) == (1, 0):
            relay(1, 1)
        remote(sq_recv.at[t, tile], sq_recv.at[t, tile], q_send.at[t, tile], q_recv.at[t, tile], sib).wait_recv()
        squares = jnp.sum(sq_mine[rows, :] + sq_recv[t, tile], axis=1, keepdims=True)
        scale = jnp.broadcast_to(lax.rsqrt(squares * (1.0 / 4096) + EPS), (SEG, 128))
        for p in range(2):
            land = part_recv.at[t, tile, p]
            remote(land, land, p_send.at[t, tile, p], p_recv.at[t, tile, p], sib).wait_recv()
            whole = own_part[p] + part_recv[t, tile, p].astype(F32)
            cols = piece_cols(c, p)
            panel = hid[t, tile, :, cols].astype(F32) + by_rows(whole, scale)
            if t < 2:
                entering = fd[t, tile, :, p * PIECE : (p + 1) * PIECE].astype(F32)
                pan_send[t, tile, p] = jnp.where(layer == 7, entering, panel).astype(BF16)
                remote(
                    pan_send.at[t, tile, p], hid.at[t + 1, tile, :, cols], n_send.at[t, tile, p], n_recv.at[t, tile, p], up
                ).start()
            else:
                pan_stage[tile, p] = panel.astype(BF16)

                @pl.when(c == tile)
                def _():
                    pltpu.make_async_copy(pan_stage.at[tile, p], panel_out.at[:, cols], o_loc.at[p]).start()

                @pl.when(c != tile)
                def _():
                    remote(pan_stage.at[tile, p], panel_out.at[:, cols], o_send.at[p], o_recv.at[p], sib).start()

    def relay(t, tile):
        for p in range(2):
            part = hid.at[t, tile, :, piece_cols(c, p)]
            remote(part, part, n_send.at[t - 1, tile, p], n_recv.at[t - 1, tile, p], up).wait_recv()
            remote(part, part, r_send.at[t - 1, tile, p], r_recv.at[t - 1, tile, p], sib).start()

    def receive(t, tile):
        for p in range(2):
            ingest(t, tile, c * 2 + p)
        for p in range(2):
            part = hid.at[t, tile, :, piece_cols(oc, p)]
            remote(part, part, r_send.at[t - 1, tile, p], r_recv.at[t - 1, tile, p], sib).wait_recv()
            ingest(t, tile, oc * 2 + p)

    ssq[...] = jnp.zeros((2 * SEG, 128), F32)

    @pl.loop(0, 2 * PIECES)
    def _(i):
        ingest(0, lax.rem(i, 2), lax.div(i, 2))

    second_x(bc_part, 8)

    @pl.loop(0, STEPS // 2)
    def _(i):
        second_x(part_of(2 * i), 2 * i)
        second_g(part_of(2 * i + 1), 2 * i + 1)

    third_x(bc_part, 8)

    @pl.loop(0, STEPS // 2)
    def _(i):
        third_x(part_of(2 * i), 2 * i)
        third_g(part_of(2 * i + 1), 2 * i + 1)

    last_x(bc_part, 8)
    for tile in range(2):
        prologue(0, tile)

    @pl.loop(0, STEPS)
    def _(q):
        @pl.when(lax.rem(q, 2) == 0)
        def _():
            last_x(part_of(q), q)

        @pl.when(lax.rem(q, 2) == 1)
        def _():
            last_g(part_of(q), q)

        project(0, q, made_a)
        project(1, q, made_b)
        step_of(0, 0, q, made_a)
        step_of(0, 1, q, made_b)
        state_off(0, 1, q)

    for tile in range(2):
        emit(0, tile)

    for t in (1, 2):
        for tile in range(2):
            ssq[tile * SEG : (tile + 1) * SEG, :] = jnp.zeros((SEG, 128), F32)
            if (t, tile) != (1, 1):
                relay(t, tile)
            receive(t, tile)
            prologue(t, tile)

            project(tile, 0, made_a)

            @pl.loop(0, STEPS // 2)
            def _(i):
                q = 2 * i
                if tile == 0:
                    state_arrived(t, q)
                    state_arrived(t, q + 1)
                project(tile, q + 1, made_b)
                step_of(t, tile, q, made_a)
                project(tile, lax.rem(q + 2, STEPS), made_a)
                step_of(t, tile, q + 1, made_b)
                state_off(t, tile, q)
                state_off(t, tile, q + 1)

            emit(t, tile)

    sent(bc_landed(), 8, 18)
    sent_x(bc_part, 8)

    @pl.loop(0, STEPS)
    def _(q):
        sent(main_landed(q), q, 18)

        @pl.when(lax.rem(q, 2) == 0)
        def _():
            sent_x(part_of(q), q)

        @pl.when(lax.rem(q, 2) == 1)
        def _():
            sent_g(part_of(q), q)

        place = state_out.at[pl.ds(mult(c * HALF + q * CHUNK, CHUNK), CHUNK), :]
        land = state_out.at[pl.ds(mult(oc * HALF + q * CHUNK, CHUNK), CHUNK), :]
        turned_q = pl.ds(mult(q * CHUNK, CHUNK), CHUNK)
        pltpu.make_async_copy(s_in.at[c, turned_q, :], place, f_loc.at[q]).wait()
        remote(s_in.at[oc, turned_q, :], land, f_send.at[q], f_recv.at[q], sib).wait()
        for t in range(2):
            remote(s_send.at[t, q], s_recv.at[t, q], st_send.at[t, q], st_recv.at[t, q], after).wait_send()

    for src, dst, i in begin:
        remote(src, dst, m_send.at[i], m_recv.at[i], sib).wait_send()
    for t in range(2):
        remote(bc_to.at[t], bc_from.at[t], m_send.at[4 + t], m_recv.at[4 + t], after).wait_send()

    for p in range(2):
        pltpu.make_async_copy(pan_stage.at[c, p], panel_out.at[:, piece_cols(c, p)], o_loc.at[p]).wait()
        remote(pan_stage.at[oc, p], panel_out.at[:, piece_cols(oc, p)], o_send.at[p], o_recv.at[p], sib).wait()

    @pl.loop(0, 2)
    def _(tile):
        for t in range(3):
            remote(sq_send.at[t, tile], sq_recv.at[t, tile], q_send.at[t, tile], q_recv.at[t, tile], sib).wait_send()
            for p in range(2):
                src, dst = part_send.at[t, tile, p], part_recv.at[t, tile, p]
                remote(src, dst, p_send.at[t, tile, p], p_recv.at[t, tile, p], sib).wait_send()
        for t in range(2):
            for p in range(2):
                part = hid.at[t + 1, tile, :, piece_cols(c, p)]
                remote(pan_send.at[t, tile, p], part, n_send.at[t, tile, p], n_recv.at[t, tile, p], up).wait_send()
                remote(part, part, r_send.at[t, tile, p], r_recv.at[t, tile, p], sib).wait_send()


def hand_over(panel, state, panel_out, state_out, panel_here, state_here, sem_in, sem_out):
    pieces = [(panel, panel_here, panel_out)]
    for i in range(4):
        rows = pl.ds(i * 1024, 1024)
        pieces.append((state.at[rows, :], state_here.at[rows, :], state_out.at[rows, :]))
    for i, (src, here, _) in enumerate(pieces):
        pltpu.make_async_copy(src, here, sem_in.at[i]).start()
    for i, (src, here, dst) in enumerate(pieces):
        pltpu.make_async_copy(src, here, sem_in.at[i]).wait()
        pltpu.make_async_copy(here, dst, sem_out.at[i]).start()
    for i, (_, here, dst) in enumerate(pieces):
        pltpu.make_async_copy(here, dst, sem_out.at[i]).wait()


def local(
    panels, feed, ssm_state, conv_state, w_in, w_out, norm_gain, conv_weight, conv_bias,
    dt_bias, decay_rate, skip_gain, out_gain,
):
    any_ = pl.BlockSpec(memory_space=pl.ANY)
    vmem = pl.BlockSpec(memory_space=pltpu.VMEM)
    dma = pltpu.SemaphoreType.DMA
    scratch = [
        pltpu.VMEM((9280, 128), BF16),
        pltpu.VMEM((STEPS, 128, 512), BF16),
        pltpu.VMEM((128, 640), BF16),
        pltpu.VMEM((8, 128), F32),
        pltpu.VMEM((STEPS, 2048, 512), BF16),
        pltpu.VMEM((2048, 640), BF16),
        pltpu.VMEM((HALF, WIDTH), BF16),
        pltpu.VMEM((3, 2, SEG, WIDTH), BF16),
        pltpu.VMEM((2 * SEG, WIDTH), BF16),
        pltpu.VMEM((2 * SEG, 128), F32),
        pltpu.VMEM((2 * SEG, 128), F32),
        pltpu.VMEM((2, 8, 5120), F32),
        pltpu.VMEM((2, STEPS, 8, CHUNK), F32),
        pltpu.VMEM((2, 8, 512), F32),
        pltpu.VMEM((2, 16, 512), BF16),
        pltpu.VMEM((2, 16, 512), BF16),
        pltpu.VMEM((2, HALF, 128), F32),
        pltpu.VMEM((2, STEPS, 128, CHUNK), F32),
        pltpu.VMEM((2, STEPS, 144, CHUNK), BF16),
        pltpu.VMEM((2, STEPS, 144, CHUNK), BF16),
        pltpu.VMEM((2, 2, SEG, 1024), BF16),
        pltpu.VMEM((4, SEG + 8, 128), F32),
        pltpu.VMEM((SEG, 640), F32),
        pltpu.VMEM((SEG, 512), F32),
        pltpu.VMEM((SEG, 512), F32),
        pltpu.VMEM((2, 2, SEG, 128), BF16),
        pltpu.VMEM((2, 2, SEG, 128), BF16),
        pltpu.VMEM((2, 2, SEG, 128), F32),
        pltpu.VMEM((2, 2, 32, 32), F32),
        pltpu.VMEM((2, SEG, 128), F32),
        pltpu.VMEM((2, 128, 256), F32),
        pltpu.VMEM((4 * SEG, 128), BF16),
        pltpu.VMEM((2, 8, 128), F32),
        pltpu.VMEM((2 * SEG, HALF), BF16),
        pltpu.VMEM((2, SEG, PIECE), F32),
        pltpu.VMEM((3, 2, 2, SEG, PIECE), BF16),
        pltpu.VMEM((3, 2, 2, SEG, PIECE), BF16),
        pltpu.VMEM((2 * SEG, 128), F32),
        pltpu.VMEM((3, 2, SEG, 128), F32),
        pltpu.VMEM((3, 2, SEG, 128), F32),
        pltpu.VMEM((2, 2, 2, SEG, PIECE), BF16),
        pltpu.VMEM((2, 2, SEG, PIECE), BF16),
        dma((9, 19)), dma((9, 19)), dma((7,)), dma((6,)), dma((6,)), dma((3, 2, 2)), dma((3, 2, 2)),
        dma((2, 2, 2)), dma((2, 2, 2)), dma((2, 2, 2)), dma((2, 2, 2)),
        dma((2, STEPS)), dma((2, STEPS)), dma((STEPS,)), dma((STEPS,)), dma((STEPS,)),
        dma((3, 2)), dma((3, 2)), dma((2,)), dma((2,)), dma((2,)),
    ]
    panel, state = pl.pallas_call(
        kernel,
        out_shape=(
            jax.ShapeDtypeStruct((SEG, WIDTH), BF16),
            jax.ShapeDtypeStruct((4096, 128), F32),
        ),
        in_specs=[any_] * 5 + [vmem] * 8,
        out_specs=(any_, any_),
        scratch_shapes=scratch,
        compiler_params=pltpu.CompilerParams(
            collective_id=0, has_side_effects=True, vmem_limit_bytes=60 * 1024 * 1024
        ),
        cost_estimate=pl.CostEstimate(flops=28_000_000_000, bytes_accessed=60_000_000, transcendentals=20_000_000),
    )(
        panels[0], feed, ssm_state.reshape(4096, 128), w_in[0].T, w_out[0], conv_state[0, 0],
        norm_gain, conv_weight[0], conv_bias, dt_bias, decay_rate, skip_gain, out_gain,
    )
    panel, state = pl.pallas_call(
        hand_over,
        out_shape=(jax.ShapeDtypeStruct((SEG, WIDTH), BF16), jax.ShapeDtypeStruct((4096, 128), F32)),
        in_specs=[any_, any_],
        out_specs=(any_, any_),
        scratch_shapes=[pltpu.VMEM((SEG, WIDTH), BF16), pltpu.VMEM((4096, 128), F32), dma((5,)), dma((5,))],
        compiler_params=pltpu.CompilerParams(vmem_limit_bytes=60 * 1024 * 1024),
    )(panel, state)
    return (panel[None], state.reshape(1, 1, 64, 64, 128))


def solution(mesh):
    return jax.shard_map(
        local,
        mesh=mesh,
        in_specs=(
            P("layer", "seq", None),
            P(None, "seq", None),
            P("layer", "seq", None, None, None),
            P("layer", "seq", None, None),
            P("layer", "seq", None),
            P("layer", None, None),
            P("layer", None),
            P("layer", None, None),
            P("layer", None),
            P("layer", None),
            P("layer", None),
            P("layer", None),
            P("layer", None),
        ),
        out_specs=(P("layer", "seq", None), P("layer", "seq", None, None, None)),
        check_vma=False,
    )
```

```python
import functools

import jax
import jax.numpy as jnp
from jax import lax
from jax.experimental import pallas as pl
from jax.experimental.pallas import tpu as pltpu
from jax.sharding import PartitionSpec as P

EPS = 1e-05
LOG2E = 1.4426950408889634
F32 = jnp.float32
BF16 = jnp.bfloat16
SEG = 160
WIDTH = 2048
HALF = 2048
CHUNK = 256
STEPS = HALF // CHUNK
PIECE = 512
PIECES = WIDTH // PIECE
MESH = pl.DeviceIdType.MESH


def silu_of_half(half):
    return half + half * jnp.tanh(half)


def dot(a, b):
    return jnp.dot(a, b, preferred_element_type=F32)


def by_rows(v, scale):
    blocks = [v[:, i : i + 128] * scale for i in range(0, v.shape[1], 128)]
    return blocks[0] if len(blocks) == 1 else jnp.concatenate(blocks, axis=1)


def lane_sums(v):
    total = v[:, :128]
    for i in range(128, v.shape[1], 128):
        total = total + v[:, i : i + 128]
    return total


def kernel(
    panels, feed, state_in, w_in, w_out, tail_in, norm_gain, conv_w, conv_b, dt_bias, decay_rate, skip_gain, out_gain,
    panel_out, state_out,
    w_rows, w_cut, bc_cut, heads,
    w_main, w_bc, w_o, hid, hg, ssq, rowscale, tails, x_loc, bc_loc, bc_to, bc_from, s_in, s_loc, s_send, s_recv, fd,
    convbuf, proj, made_a, made_b, b_all, c_all, score_a, score_b, ld_col, ld_row, e_all, e_fin,
    gated, own_part, part_send, part_recv, sq_mine, sq_send, sq_recv, pan_send, pan_stage,
    g_send, g_recv, l_sem, m_send, m_recv, p_send, p_recv, n_send, n_recv, r_send, r_recv,
    st_send, st_recv, f_send, f_recv, f_loc, q_send, q_recv, o_send, o_recv, o_loc,
):
    layer = lax.axis_index("layer")
    seq = lax.axis_index("seq")
    c = lax.rem(seq, 2)
    m = lax.div(seq, 2)
    y = lax.rem(m, 4)
    z = lax.div(m, 4)
    oc = 1 - c
    yp = lax.rem(y + 1, 4)
    ym = lax.rem(y + 3, 4)
    y2 = lax.rem(y + 2, 4)
    oz = 1 - z

    def at(zz, yy, cc):
        return (layer, zz * 8 + yy * 2 + cc)

    sib = at(z, y, oc)
    to_yp = at(z, yp, c)
    to_ym = at(z, ym, c)
    to_z = at(oz, y, c)
    up = (lax.rem(layer + 1, 8), seq)
    down = (lax.rem(layer + 7, 8), seq)
    after = (layer, lax.rem(seq + 2, 16))
    before = (layer, lax.rem(seq + 14, 16))

    def mult(v, by):
        return pl.multiple_of(v, by)

    local = (
        (w_in.at[pl.ds(8192, 1088), :], w_rows.at[pl.ds(8192, 1088), :]),
        (w_in.at[pl.ds(4096, 4096), :], w_rows.at[pl.ds(4096, 4096), :]),
        (w_in.at[pl.ds(0, 4096), :], w_rows.at[pl.ds(0, 4096), :]),
        (panels, hid.at[0, c]),
        (state_in.at[pl.ds(mult(c * HALF, HALF), HALF), :], s_in.at[c]),
        (w_out.at[pl.ds(mult(c * HALF, HALF), HALF), :], w_o),
        (feed.at[:, :, pl.ds(mult(c * 1024, 1024), 1024)], fd.at[:, c]),
    )
    for i, (src, dst) in enumerate(local[:3]):
        pltpu.make_async_copy(src, dst, l_sem.at[i]).start()

    barrier = pltpu.get_barrier_semaphore()
    friends = (sib, to_yp, to_ym, to_z, up, down, after, before)
    for friend in friends:
        pl.semaphore_signal(barrier, inc=1, device_id=friend, device_id_type=MESH)

    heads[...] = jnp.zeros((8, 128), F32)
    heads[0:1, 0:64] = dt_bias[...]
    heads[1:2, 0:64] = decay_rate[...]
    heads[2:3, 0:64] = skip_gain[...]
    tails[c, 0:8, :] = jnp.zeros((8, 5120), F32)
    tails[c, 5:8, :] = tail_in[...].astype(F32)

    for i, (src, dst) in enumerate(local[:3]):
        pltpu.make_async_copy(src, dst, l_sem.at[i]).wait()
    pl.semaphore_wait(barrier, len(friends))

    def remote(src, dst, ss, rs, who):
        return pltpu.make_async_remote_copy(
            src_ref=src, dst_ref=dst, send_sem=ss, recv_sem=rs, device_id=who, device_id_type=MESH
        )

    own_rows = mult(m * 256 + c * 128, 128)
    sib_rows = mult(m * 256 + oc * 128, 128)

    def turned(start, size):
        return w_rows[pl.ds(mult(start, 64), size), :].T

    def bc_prepare():
        dt = jnp.concatenate([turned(9216, 64), jnp.zeros((128, 64), BF16)], axis=1)
        rows = pl.ds(own_rows, 128)
        for cc, target, where in ((c, w_bc, rows), (oc, bc_cut, slice(0, 128))):
            target[where, 0:256] = turned(8192 + cc * 256, 256)
            target[where, 256:512] = turned(8704 + cc * 256, 256)
            target[where, 512:640] = dt
        remote(bc_cut, w_bc.at[rows, :], g_send.at[8, 18], g_recv.at[8, 18], sib).start()
        push(bc_part(m, c), 8, 2, to_z)
        push(bc_part(m, c), 8, 0, to_yp)
        push(bc_part(m, c), 8, 1, to_ym)

    def main_prepare(q):
        rows = pl.ds(own_rows, 128)
        w_main[q, rows, 0:256] = turned(4096 + c * 2048 + q * 256, 256)
        w_main[q, rows, 256:512] = turned(c * 2048 + q * 256, 256)
        w_cut[q, :, 0:256] = turned(4096 + oc * 2048 + q * 256, 256)
        w_cut[q, :, 256:512] = turned(oc * 2048 + q * 256, 256)
        remote(w_cut.at[q], w_main.at[q, rows, :], g_send.at[q, 18], g_recv.at[q, 18], sib).start()

    def bc_landed():
        return w_bc.at[pl.ds(sib_rows, 128), :]

    def main_landed(q):
        return w_main.at[q, pl.ds(sib_rows, 128), :]

    def bc_part(mm, half=None):
        if half is None:
            return w_bc.at[pl.ds(mult(mm * 256, 256), 256), :]
        return w_bc.at[pl.ds(mult(mm * 256 + half * 128, 128), 128), :]

    def main_part(q, mm, half=None):
        if half is None:
            return w_main.at[q, pl.ds(mult(mm * 256, 256), 256), :]
        return w_main.at[q, pl.ds(mult(mm * 256 + half * 128, 128), 128), :]

    def part_of(q):
        return functools.partial(main_part, q)

    m_yp, m_ym, m_y2 = z * 4 + yp, z * 4 + ym, z * 4 + y2
    o_y, o_yp, o_ym, o_y2 = oz * 4 + y, oz * 4 + yp, oz * 4 + ym, oz * 4 + y2

    def push(part, q, slot, who):
        remote(part, part, g_send.at[q, slot], g_recv.at[q, slot], who).start()

    def arrived(part, q, slot):
        remote(part, part, g_send.at[q, slot], g_recv.at[q, slot], sib).wait_recv()

    def sent(part, q, slot):
        remote(part, part, g_send.at[q, slot], g_recv.at[q, slot], sib).wait_send()

    def first_x(part, q):
        push(part(m), q, 2, to_z)
        push(part(m), q, 0, to_yp)
        push(part(m), q, 1, to_ym)

    def first_g(part, q):
        push(part(m), q, 5, to_z)
        push(part(m), q, 3, to_yp)
        push(part(m), q, 4, to_ym)

    def landed_first(part, q, mm, slot):
        if part is bc_part:
            arrived(part(mm, c), q, slot)
            arrived(part(mm, oc), q, slot + 3)
        else:
            arrived(part(mm), q, slot)

    def second_x(part, q):
        landed_first(part, q, o_y, 2)
        push(part(o_y), q, 6, to_yp)
        push(part(o_y), q, 7, to_ym)
        landed_first(part, q, m_ym, 0)
        push(part(m_ym, 0), q, 8, to_yp)
        landed_first(part, q, m_yp, 1)
        push(part(m_yp, 1), q, 9, to_ym)

    def second_g(part, q):
        arrived(part(m_ym), q, 3)
        push(part(m_ym), q, 11, to_z)
        push(part(m_ym, 0), q, 10, to_yp)
        arrived(part(m_yp), q, 4)
        push(part(m_yp), q, 13, to_z)
        push(part(m_yp, 1), q, 12, to_ym)
        arrived(part(o_y), q, 5)

    def third_x(part, q):
        arrived(part(o_ym), q, 6)
        push(part(o_ym, 0), q, 14, to_yp)
        arrived(part(o_yp), q, 7)
        push(part(o_yp, 1), q, 15, to_ym)
        arrived(part(m_y2, 0), q, 8)
        arrived(part(m_y2, 1), q, 9)

    def third_g(part, q):
        arrived(part(m_y2, 0), q, 10)
        push(part(m_y2, 0), q, 16, to_z)
        arrived(part(m_y2, 1), q, 12)
        push(part(m_y2, 1), q, 17, to_z)
        arrived(part(o_ym), q, 11)
        arrived(part(o_yp), q, 13)

    def last_x(part, q):
        arrived(part(o_y2, 0), q, 14)
        arrived(part(o_y2, 1), q, 15)

    def last_g(part, q):
        arrived(part(o_y2, 0), q, 16)
        arrived(part(o_y2, 1), q, 17)

    def sent_x(part, q):
        for slot in (0, 1, 2):
            if part is bc_part:
                sent(part(m, 0), q, slot)
                sent(part(m, 0), q, slot + 3)
            else:
                sent(part(m), q, slot)
        for slot in (6, 7):
            sent(part(m), q, slot)
        for slot in (8, 9, 14, 15):
            sent(part(m, 0), q, slot)

    def sent_g(part, q):
        for slot in (3, 4, 5, 11, 13):
            sent(part(m), q, slot)
        for slot in (10, 12, 16, 17):
            sent(part(m, 0), q, slot)

    bc_prepare()
    main_prepare(0)
    arrived(bc_landed(), 8, 18)
    push(bc_part(m, oc), 8, 5, to_z)
    push(bc_part(m, oc), 8, 3, to_yp)
    push(bc_part(m, oc), 8, 4, to_ym)

    @pl.loop(0, STEPS // 2)
    def _(i):
        q = 2 * i
        main_prepare(q + 1)
        arrived(main_landed(q), q, 18)
        first_x(part_of(q), q)

        @pl.when(i < STEPS // 2 - 1)
        def _():
            main_prepare(q + 2)

        arrived(main_landed(q + 1), q + 1, 18)
        first_g(part_of(q + 1), q + 1)

    begin = (
        (panels, hid.at[0, c], 0),
        (tails.at[c], tails.at[c], 1),
        (state_in.at[pl.ds(mult(oc * HALF, HALF), HALF), :], s_in.at[c], 2),
        (feed.at[:, :, pl.ds(mult(oc * 1024, 1024), 1024)], fd.at[:, c], 3),
    )
    for src, dst, i in begin:
        remote(src, dst, m_send.at[i], m_recv.at[i], sib).start()
    for i, (src, dst) in enumerate(local[3:]):
        pltpu.make_async_copy(src, dst, l_sem.at[3 + i]).start()
    for i, (src, dst) in enumerate(local[3:]):
        pltpu.make_async_copy(src, dst, l_sem.at[3 + i]).wait()
    for (src, dst, i), land in zip(begin, (hid.at[0, oc], tails.at[oc], s_in.at[oc], fd.at[:, oc])):
        remote(land, land, m_send.at[i], m_recv.at[i], sib).wait_recv()

    def ingest(t, tile, n):
        cols = pl.ds(mult(n * PIECE, PIECE), PIECE)
        rows = pl.ds(mult(tile * SEG, 32), SEG)
        h = hid[t, tile, :, cols].astype(F32)
        ssq[rows, :] += lane_sums(h * h)
        hg[rows, cols] = (h * norm_gain[:, cols]).astype(BF16)

    lane = lax.broadcasted_iota(jnp.int32, (SEG, 128), 1)
    row = lax.broadcasted_iota(jnp.int32, (SEG, 128), 0)

    def conv(slot, tile_tail, fresh, weight, bias):
        convbuf[slot, 0:8, :] = tile_tail
        convbuf[slot, 8 : 8 + SEG, :] = fresh
        total = bias
        for k in range(4):
            total = total + convbuf[slot, 5 + k : 5 + k + SEG, :] * weight[k : k + 1, :]
        return silu_of_half(total).astype(BF16)

    def x_tail(t, tile, q, pair, cols):
        lanes = slice(pair * 128, pair * 128 + 128)
        if t == 0:
            return tails[tile, :, cols]
        if tile == 1:
            return x_loc[t - 1, q, :, lanes]
        return jnp.where(m > 0, s_recv[t - 1, q, 128:144, lanes].astype(F32)[8:16], 0.0)

    def bc_tail(t, tile, block, cols):
        lanes = slice(block * 128, block * 128 + 128)
        if t == 0:
            return tails[tile, :, cols]
        if tile == 1:
            return bc_loc[t - 1, :, lanes]
        return jnp.where(m > 0, bc_from[t - 1, :, lanes].astype(F32)[8:16], 0.0)

    def keep_tail(t, tile, slot, here, away):
        if t < 2 and tile == 0:
            target, at_ = here
            target[at_] = convbuf[slot, SEG : SEG + 8, :]
        elif t < 2:
            target, at_ = away
            target[at_] = convbuf[slot, SEG - 8 : SEG + 8, :].astype(BF16)

    def prologue(t, tile):
        rows = slice(tile * SEG, (tile + 1) * SEG)
        if t > 0 and tile == 0:
            remote(bc_to.at[t - 1], bc_from.at[t - 1], m_send.at[3 + t], m_recv.at[3 + t], after).wait_recv()
        total = jnp.sum(ssq[rows, :], axis=1, keepdims=True)
        rowscale[rows, :] = jnp.broadcast_to(lax.rsqrt(total * (1.0 / WIDTH) + EPS), (SEG, 128))
        proj[...] = dot(hg[rows, :], w_bc[...])
        causal = lane <= row
        tri = (
            lax.broadcasted_iota(jnp.int32, (SEG, SEG), 1) <= lax.broadcasted_iota(jnp.int32, (SEG, SEG), 0)
        ).astype(BF16)
        sq_mine[rows, :] = jnp.zeros((SEG, 128), F32)
        scale = rowscale[rows, :]
        for block in range(4):
            slot = block % 2
            base = 4096 if block < 2 else 4608
            cols = pl.ds(mult(base + c * 256 + slot * 128, 128), 128)
            fresh = proj[:, block * 128 : block * 128 + 128] * scale
            made = conv(
                tile * 2 + slot, bc_tail(t, tile, block, cols), fresh, 0.5 * conv_w[:, cols], 0.5 * conv_b[:, cols]
            )
            lanes = slice(block * 128, block * 128 + 128)
            keep_tail(t, tile, tile * 2 + slot, (bc_loc, (min(t, 1), slice(0, 8), lanes)), (bc_to, (min(t, 1), slice(0, 16), lanes)))
            target = b_all if block < 2 else c_all
            target[tile, slot] = made
        for g in range(2):
            scores = lax.dot_general(
                c_all[tile, g], b_all[tile, g], (((1,), (1,)), ((), ())), preferred_element_type=F32
            )
            score_a[tile, g] = jnp.where(causal, scores[:, 0:128], 0.0)
            score_b[tile, g] = jnp.where(causal[0:32, 0:32], scores[128:SEG, 128:SEG], 0.0)
        v = proj[:, 512:640] * scale + heads[0:1, :]
        step = jnp.maximum(v, 0.0) + jnp.log1p(jnp.exp(-jnp.abs(v)))
        fall = -heads[1:2, :] * step
        coarse = fall.astype(BF16)
        rest = fall - coarse.astype(F32)
        fine = rest.astype(BF16)
        finest = (rest - fine.astype(F32)).astype(BF16)
        sums = dot(tri, jnp.concatenate([coarse, fine, finest], axis=1))
        ld = sums[:, 0:128] + (sums[:, 128:256] + sums[:, 256:384])
        last = ld[SEG - 1 : SEG, :]
        ld_col[tile] = ld * LOG2E
        ld_row[tile, :, 0:SEG] = (ld * LOG2E - jnp.log2(step)).T
        e_all[2 * tile * SEG : (2 * tile + 1) * SEG, :] = jnp.exp(ld).astype(BF16)
        e_all[(2 * tile + 1) * SEG : (2 * tile + 2) * SEG, :] = (jnp.exp(last - ld) * step).astype(BF16)
        e_fin[tile, 0:1, :] = jnp.exp(last)
        e_fin[tile, 1:2, :] = heads[2:3, :]

        if t < 2 and tile == 1:
            remote(bc_to.at[t], bc_from.at[t], m_send.at[4 + t], m_recv.at[4 + t], after).start()

    low = lane < 64

    def project(tile, q, into, half):
        cols = slice(half * 256, half * 256 + 256)
        into[:, cols] = dot(hg[tile * SEG : (tile + 1) * SEG, :], w_main[q, :, cols])

    def state_arrived(t, q):
        land = s_recv.at[t - 1, q]
        remote(land, land, st_send.at[t - 1, q], st_recv.at[t - 1, q], after).wait_recv()

    def step_of(t, tile, q, made_of, beside):
        beside(0)
        rows = slice(tile * SEG, (tile + 1) * SEG)
        g = lax.div(q, 4)
        base = c * 32 + q * 4
        first = lax.rem(128 - base, 128)
        spread = (
            lax.broadcasted_iota(jnp.int32, (128, CHUNK), 0)
            == base + lax.div(lax.broadcasted_iota(jnp.int32, (128, CHUNK), 1), 64)
        ).astype(F32)
        both_e = slice(2 * tile * SEG, (2 * tile + 2) * SEG)
        spread_out = dot(e_all[both_e, :], spread.astype(BF16))
        scale = rowscale[rows, :]
        half_scale = 0.5 * scale
        if t == 0:
            state = s_in[tile, pl.ds(mult(q * CHUNK, CHUNK), CHUNK), :].T
        elif tile == 0:
            state = jnp.where(m > 0, s_recv[t - 1, q, 0:128, :].astype(F32), 0.0)
        else:
            state = s_loc[t - 1, q]
        ld = pltpu.roll(ld_col[tile], first, 1)
        ends = pltpu.roll(e_fin[tile], first, 1)
        sa, sb = score_a[tile, g], score_b[tile, g]
        carried = dot(c_all[tile, g], state.astype(BF16))
        squares = jnp.zeros((SEG, 128), F32)
        grown = []
        xs = []
        for pair in range(2):
            lanes = slice(pair * 128, pair * 128 + 128)
            cols = pl.ds(mult(c * HALF + q * CHUNK + pair * 128, 128), 128)
            slot = tile * 2 + pair
            x = conv(
                slot, x_tail(t, tile, q, pair, cols), made_of[:, lanes] * scale, 0.5 * conv_w[:, cols], 0.5 * conv_b[:, cols]
            )
            keep_tail(t, tile, slot, (x_loc, (min(t, 1), q, slice(0, 8), lanes)), (s_send, (min(t, 1), q, slice(128, 144), lanes)))
            xs.append(x)
        beside(1)
        for pair in range(2):
            lanes = slice(pair * 128, pair * 128 + 128)
            cols = pl.ds(mult(c * HALF + q * CHUNK + pair * 128, 128), 128)
            x = xs[pair]
            weights = []
            for h in (pair * 2, pair * 2 + 1):
                col = jnp.broadcast_to(ld[:, h : h + 1], (SEG, 128))
                ldr = ld_row[tile, pl.ds(base + h, 1), :]
                wa = (sa * jnp.exp2(jnp.minimum(col - ldr[:, 0:128], 64.0))).astype(BF16)
                wb = (sb * jnp.exp2(jnp.minimum(col[128:SEG, 0:32] - ldr[:, 128:SEG], 64.0))).astype(BF16)
                wb = jnp.concatenate([jnp.zeros((128, 32), BF16), wb], axis=0)
                weights.append(jnp.concatenate([wa, wb], axis=1))
            both = dot(jnp.concatenate(weights, axis=0), x)
            mixed = jnp.where(low, both[0:SEG], both[SEG : 2 * SEG])
            wide = x.astype(F32)
            end = jnp.where(low[0:8], ends[:, 2 * pair : 2 * pair + 1], ends[:, 2 * pair + 1 : 2 * pair + 2])
            e_now = spread_out[0:SEG, lanes]
            e_last = spread_out[SEG : 2 * SEG, lanes]
            combined = mixed + carried[:, lanes] * e_now + end[1:2, :] * wide
            gate = slice(CHUNK + pair * 128, CHUNK + pair * 128 + 128)
            out = combined * silu_of_half(made_of[:, gate] * half_scale)
            squares = squares + out * out
            gated[rows, pl.ds(mult(q * CHUNK + pair * 128, 128), 128)] = (out * out_gain[:, cols]).astype(BF16)
            grew = lax.dot_general(
                b_all[tile, g], (wide * e_last).astype(BF16), (((0,), (0,)), ((), ())), preferred_element_type=F32
            )
            grown.append(end[0:1, :] * state[:, lanes] + grew)
        sq_mine[rows, :] += squares
        made = jnp.concatenate(grown, axis=1)
        if t < 2 and tile == 0:
            s_loc[t, q] = made
        elif t < 2:
            s_send[t, q, 0:128, :] = made.astype(BF16)
        else:
            s_in[tile, pl.ds(mult(q * CHUNK, CHUNK), CHUNK), :] = made.T

    def state_off(t, tile, q):
        if t < 2 and tile == 1:
            remote(s_send.at[t, q], s_recv.at[t, q], st_send.at[t, q], st_recv.at[t, q], after).start()
        elif t == 2:
            place = state_out.at[pl.ds(mult(c * HALF + q * CHUNK, CHUNK), CHUNK), :]
            turned_q = pl.ds(mult(q * CHUNK, CHUNK), CHUNK)

            @pl.when(c == tile)
            def _():
                pltpu.make_async_copy(s_in.at[tile, turned_q, :], place, f_loc.at[q]).start()

            @pl.when(c != tile)
            def _():
                remote(s_in.at[tile, turned_q, :], place, f_send.at[q], f_recv.at[q], sib).start()

    def piece_cols(half, p):
        return pl.ds(mult(half * 1024 + p * PIECE, PIECE), PIECE)

    def panel_off(t, tile, p):
        there = hid.at[t + 1, tile, :, piece_cols(c, p)]
        remote(pan_send.at[t, tile, p], there, n_send.at[t, tile, p], n_recv.at[t, tile, p], up).start()

    def emit(t, tile):
        rows = slice(tile * SEG, (tile + 1) * SEG)
        sq_send[t, tile] = sq_mine[rows, :]
        remote(sq_send.at[t, tile], sq_recv.at[t, tile], q_send.at[t, tile], q_recv.at[t, tile], sib).start()

        for p in range(2):
            part_send[t, tile, p] = dot(gated[rows, :], w_o[:, piece_cols(oc, p)]).astype(BF16)
            remote(
                part_send.at[t, tile, p], part_recv.at[t, tile, p], p_send.at[t, tile, p], p_recv.at[t, tile, p], sib
            ).start()

        for p in range(2):
            own_part[p] = dot(gated[rows, :], w_o[:, piece_cols(c, p)])

        if (t, tile) == (1, 0):
            relay(1, 1)
        remote(sq_recv.at[t, tile], sq_recv.at[t, tile], q_send.at[t, tile], q_recv.at[t, tile], sib).wait_recv()
        squares = jnp.sum(sq_mine[rows, :] + sq_recv[t, tile], axis=1, keepdims=True)
        scale = jnp.broadcast_to(lax.rsqrt(squares * (1.0 / 4096) + EPS), (SEG, 128))
        for p in range(2):
            land = part_recv.at[t, tile, p]
            remote(land, land, p_send.at[t, tile, p], p_recv.at[t, tile, p], sib).wait_recv()
            whole = own_part[p] + part_recv[t, tile, p].astype(F32)
            cols = piece_cols(c, p)
            panel = hid[t, tile, :, cols].astype(F32) + by_rows(whole, scale)
            if t < 2:
                entering = fd[t, tile, :, p * PIECE : (p + 1) * PIECE].astype(F32)
                pan_send[t, tile, p] = jnp.where(layer == 7, entering, panel).astype(BF16)
                if (t, tile) != (0, 1):
                    panel_off(t, tile, p)
            else:
                pan_stage[tile, p] = panel.astype(BF16)

                @pl.when(c == tile)
                def _():
                    pltpu.make_async_copy(pan_stage.at[tile, p], panel_out.at[:, cols], o_loc.at[p]).start()

                @pl.when(c != tile)
                def _():
                    remote(pan_stage.at[tile, p], panel_out.at[:, cols], o_send.at[p], o_recv.at[p], sib).start()

    def relay(t, tile):
        for p in range(2):
            part = hid.at[t, tile, :, piece_cols(c, p)]
            remote(part, part, n_send.at[t - 1, tile, p], n_recv.at[t - 1, tile, p], up).wait_recv()
            remote(part, part, r_send.at[t - 1, tile, p], r_recv.at[t - 1, tile, p], sib).start()

    def receive(t, tile):
        for p in range(2):
            ingest(t, tile, c * 2 + p)
        for p in range(2):
            part = hid.at[t, tile, :, piece_cols(oc, p)]
            remote(part, part, r_send.at[t - 1, tile, p], r_recv.at[t - 1, tile, p], sib).wait_recv()
            ingest(t, tile, oc * 2 + p)

    ssq[...] = jnp.zeros((2 * SEG, 128), F32)

    @pl.loop(0, 2 * PIECES)
    def _(i):
        ingest(0, lax.rem(i, 2), lax.div(i, 2))

    second_x(bc_part, 8)

    @pl.loop(0, STEPS // 2)
    def _(i):
        second_x(part_of(2 * i), 2 * i)
        second_g(part_of(2 * i + 1), 2 * i + 1)

    third_x(bc_part, 8)

    @pl.loop(0, STEPS // 2)
    def _(i):
        third_x(part_of(2 * i), 2 * i)
        third_g(part_of(2 * i + 1), 2 * i + 1)

    last_x(bc_part, 8)
    for tile in range(2):
        prologue(0, tile)

    @pl.loop(0, STEPS - 1)
    def _(q):
        @pl.when(lax.rem(q, 2) == 0)
        def _():
            last_x(part_of(q), q)

        @pl.when(lax.rem(q, 2) == 1)
        def _():
            last_g(part_of(q), q)

        for half in range(2):
            project(0, q, made_a, half)
        step_of(0, 0, q, made_a, functools.partial(project, 1, q, made_b))
        step_of(0, 1, q, made_b, lambda half: None)
        state_off(0, 1, q)

    last_g(part_of(STEPS - 1), STEPS - 1)
    for tile in range(2):
        for half in range(2):
            project(tile, STEPS - 1, made_a, half)
        step_of(0, tile, STEPS - 1, made_a, lambda half: None)
        state_off(0, tile, STEPS - 1)
        emit(0, tile)

    for t in (1, 2):
        for tile in range(2):
            ssq[tile * SEG : (tile + 1) * SEG, :] = jnp.zeros((SEG, 128), F32)
            if (t, tile) != (1, 1):
                relay(t, tile)
            if (t, tile) == (1, 0):
                for p in range(2):
                    panel_off(0, 1, p)
            receive(t, tile)
            prologue(t, tile)

            for half in range(2):
                project(tile, 0, made_a, half)

            @pl.loop(0, STEPS // 2)
            def _(i):
                q = 2 * i
                if tile == 0:
                    state_arrived(t, q)
                    state_arrived(t, q + 1)
                step_of(t, tile, q, made_a, functools.partial(project, tile, q + 1, made_b))
                step_of(t, tile, q + 1, made_b, functools.partial(project, tile, lax.rem(q + 2, STEPS), made_a))
                state_off(t, tile, q)
                state_off(t, tile, q + 1)

            emit(t, tile)

    sent(bc_landed(), 8, 18)
    sent_x(bc_part, 8)

    @pl.loop(0, STEPS)
    def _(q):
        sent(main_landed(q), q, 18)

        @pl.when(lax.rem(q, 2) == 0)
        def _():
            sent_x(part_of(q), q)

        @pl.when(lax.rem(q, 2) == 1)
        def _():
            sent_g(part_of(q), q)

        place = state_out.at[pl.ds(mult(c * HALF + q * CHUNK, CHUNK), CHUNK), :]
        land = state_out.at[pl.ds(mult(oc * HALF + q * CHUNK, CHUNK), CHUNK), :]
        turned_q = pl.ds(mult(q * CHUNK, CHUNK), CHUNK)
        pltpu.make_async_copy(s_in.at[c, turned_q, :], place, f_loc.at[q]).wait()
        remote(s_in.at[oc, turned_q, :], land, f_send.at[q], f_recv.at[q], sib).wait()
        for t in range(2):
            remote(s_send.at[t, q], s_recv.at[t, q], st_send.at[t, q], st_recv.at[t, q], after).wait_send()

    for src, dst, i in begin:
        remote(src, dst, m_send.at[i], m_recv.at[i], sib).wait_send()
    for t in range(2):
        remote(bc_to.at[t], bc_from.at[t], m_send.at[4 + t], m_recv.at[4 + t], after).wait_send()

    for p in range(2):
        pltpu.make_async_copy(pan_stage.at[c, p], panel_out.at[:, piece_cols(c, p)], o_loc.at[p]).wait()
        remote(pan_stage.at[oc, p], panel_out.at[:, piece_cols(oc, p)], o_send.at[p], o_recv.at[p], sib).wait()

    @pl.loop(0, 2)
    def _(tile):
        for t in range(3):
            remote(sq_send.at[t, tile], sq_recv.at[t, tile], q_send.at[t, tile], q_recv.at[t, tile], sib).wait_send()
            for p in range(2):
                src, dst = part_send.at[t, tile, p], part_recv.at[t, tile, p]
                remote(src, dst, p_send.at[t, tile, p], p_recv.at[t, tile, p], sib).wait_send()
        for t in range(2):
            for p in range(2):
                part = hid.at[t + 1, tile, :, piece_cols(c, p)]
                remote(pan_send.at[t, tile, p], part, n_send.at[t, tile, p], n_recv.at[t, tile, p], up).wait_send()
                remote(part, part, r_send.at[t, tile, p], r_recv.at[t, tile, p], sib).wait_send()


def hand_over(panel, state, panel_out, state_out, panel_here, state_here, sem_in, sem_out):
    pieces = [(panel, panel_here, panel_out)]
    for i in range(4):
        rows = pl.ds(i * 1024, 1024)
        pieces.append((state.at[rows, :], state_here.at[rows, :], state_out.at[rows, :]))
    for i, (src, here, _) in enumerate(pieces):
        pltpu.make_async_copy(src, here, sem_in.at[i]).start()
    for i, (src, here, dst) in enumerate(pieces):
        pltpu.make_async_copy(src, here, sem_in.at[i]).wait()
        pltpu.make_async_copy(here, dst, sem_out.at[i]).start()
    for i, (_, here, dst) in enumerate(pieces):
        pltpu.make_async_copy(here, dst, sem_out.at[i]).wait()


def local(
    panels, feed, ssm_state, conv_state, w_in, w_out, norm_gain, conv_weight, conv_bias,
    dt_bias, decay_rate, skip_gain, out_gain,
):
    any_ = pl.BlockSpec(memory_space=pl.ANY)
    vmem = pl.BlockSpec(memory_space=pltpu.VMEM)
    dma = pltpu.SemaphoreType.DMA
    scratch = [
        pltpu.VMEM((9280, 128), BF16),
        pltpu.VMEM((STEPS, 128, 512), BF16),
        pltpu.VMEM((128, 640), BF16),
        pltpu.VMEM((8, 128), F32),
        pltpu.VMEM((STEPS, 2048, 512), BF16),
        pltpu.VMEM((2048, 640), BF16),
        pltpu.VMEM((HALF, WIDTH), BF16),
        pltpu.VMEM((3, 2, SEG, WIDTH), BF16),
        pltpu.VMEM((2 * SEG, WIDTH), BF16),
        pltpu.VMEM((2 * SEG, 128), F32),
        pltpu.VMEM((2 * SEG, 128), F32),
        pltpu.VMEM((2, 8, 5120), F32),
        pltpu.VMEM((2, STEPS, 8, CHUNK), F32),
        pltpu.VMEM((2, 8, 512), F32),
        pltpu.VMEM((2, 16, 512), BF16),
        pltpu.VMEM((2, 16, 512), BF16),
        pltpu.VMEM((2, HALF, 128), F32),
        pltpu.VMEM((2, STEPS, 128, CHUNK), F32),
        pltpu.VMEM((2, STEPS, 144, CHUNK), BF16),
        pltpu.VMEM((2, STEPS, 144, CHUNK), BF16),
        pltpu.VMEM((2, 2, SEG, 1024), BF16),
        pltpu.VMEM((4, SEG + 8, 128), F32),
        pltpu.VMEM((SEG, 640), F32),
        pltpu.VMEM((SEG, 512), F32),
        pltpu.VMEM((SEG, 512), F32),
        pltpu.VMEM((2, 2, SEG, 128), BF16),
        pltpu.VMEM((2, 2, SEG, 128), BF16),
        pltpu.VMEM((2, 2, SEG, 128), F32),
        pltpu.VMEM((2, 2, 32, 32), F32),
        pltpu.VMEM((2, SEG, 128), F32),
        pltpu.VMEM((2, 128, 256), F32),
        pltpu.VMEM((4 * SEG, 128), BF16),
        pltpu.VMEM((2, 8, 128), F32),
        pltpu.VMEM((2 * SEG, HALF), BF16),
        pltpu.VMEM((2, SEG, PIECE), F32),
        pltpu.VMEM((3, 2, 2, SEG, PIECE), BF16),
        pltpu.VMEM((3, 2, 2, SEG, PIECE), BF16),
        pltpu.VMEM((2 * SEG, 128), F32),
        pltpu.VMEM((3, 2, SEG, 128), F32),
        pltpu.VMEM((3, 2, SEG, 128), F32),
        pltpu.VMEM((2, 2, 2, SEG, PIECE), BF16),
        pltpu.VMEM((2, 2, SEG, PIECE), BF16),
        dma((9, 19)), dma((9, 19)), dma((7,)), dma((6,)), dma((6,)), dma((3, 2, 2)), dma((3, 2, 2)),
        dma((2, 2, 2)), dma((2, 2, 2)), dma((2, 2, 2)), dma((2, 2, 2)),
        dma((2, STEPS)), dma((2, STEPS)), dma((STEPS,)), dma((STEPS,)), dma((STEPS,)),
        dma((3, 2)), dma((3, 2)), dma((2,)), dma((2,)), dma((2,)),
    ]
    panel, state = pl.pallas_call(
        kernel,
        out_shape=(
            jax.ShapeDtypeStruct((SEG, WIDTH), BF16),
            jax.ShapeDtypeStruct((4096, 128), F32),
        ),
        in_specs=[any_] * 5 + [vmem] * 8,
        out_specs=(any_, any_),
        scratch_shapes=scratch,
        compiler_params=pltpu.CompilerParams(
            collective_id=0, has_side_effects=True, vmem_limit_bytes=60 * 1024 * 1024
        ),
        cost_estimate=pl.CostEstimate(flops=28_000_000_000, bytes_accessed=60_000_000, transcendentals=20_000_000),
    )(
        panels[0], feed, ssm_state.reshape(4096, 128), w_in[0].T, w_out[0], conv_state[0, 0],
        norm_gain, conv_weight[0], conv_bias, dt_bias, decay_rate, skip_gain, out_gain,
    )
    panel, state = pl.pallas_call(
        hand_over,
        out_shape=(jax.ShapeDtypeStruct((SEG, WIDTH), BF16), jax.ShapeDtypeStruct((4096, 128), F32)),
        in_specs=[any_, any_],
        out_specs=(any_, any_),
        scratch_shapes=[pltpu.VMEM((SEG, WIDTH), BF16), pltpu.VMEM((4096, 128), F32), dma((5,)), dma((5,))],
        compiler_params=pltpu.CompilerParams(vmem_limit_bytes=60 * 1024 * 1024),
    )(panel, state)
    return (panel[None], state.reshape(1, 1, 64, 64, 128))


def solution(mesh):
    return jax.shard_map(
        local,
        mesh=mesh,
        in_specs=(
            P("layer", "seq", None),
            P(None, "seq", None),
            P("layer", "seq", None, None, None),
            P("layer", "seq", None, None),
            P("layer", "seq", None),
            P("layer", None, None),
            P("layer", None),
            P("layer", None, None),
            P("layer", None),
            P("layer", None),
            P("layer", None),
            P("layer", None),
            P("layer", None),
        ),
        out_specs=(P("layer", "seq", None), P("layer", "seq", None, None, None)),
        check_vma=False,
    )
```

```python
import functools

import jax
import jax.numpy as jnp
from jax import lax
from jax.experimental import pallas as pl
from jax.experimental.pallas import tpu as pltpu
from jax.sharding import PartitionSpec as P

EPS = 1e-05
LOG2E = 1.4426950408889634
F32 = jnp.float32
BF16 = jnp.bfloat16
SEG = 160
WIDTH = 2048
HALF = 2048
CHUNK = 256
STEPS = HALF // CHUNK
PIECE = 512
PIECES = WIDTH // PIECE
MESH = pl.DeviceIdType.MESH


def silu_of_half(half):
    return half + half * jnp.tanh(half)


def dot(a, b):
    return jnp.dot(a, b, preferred_element_type=F32)


def by_rows(v, scale):
    blocks = [v[:, i : i + 128] * scale for i in range(0, v.shape[1], 128)]
    return blocks[0] if len(blocks) == 1 else jnp.concatenate(blocks, axis=1)


def lane_sums(v):
    total = v[:, :128]
    for i in range(128, v.shape[1], 128):
        total = total + v[:, i : i + 128]
    return total


def kernel(
    panels, feed, state_in, w_in, w_out, tail_in, norm_gain, conv_w, conv_b, dt_bias, decay_rate, skip_gain, out_gain,
    panel_out, state_out,
    w_rows, w_cut, bc_cut, heads,
    w_main, w_bc, w_o, hid, hg, ssq, rowscale, tails, x_loc, bc_loc, bc_to, bc_from, s_in, s_loc, s_send, s_recv, fd,
    convbuf, proj, made_a, made_b, b_all, c_all, score_a, score_b, ld_col, ld_row, e_all, e_fin,
    gated, own_part, part_send, part_recv, sq_mine, sq_send, sq_recv, pan_send, pan_stage,
    g_send, g_recv, l_sem, m_send, m_recv, p_send, p_recv, n_send, n_recv, r_send, r_recv,
    st_send, st_recv, f_send, f_recv, f_loc, q_send, q_recv, o_send, o_recv, o_loc,
):
    layer = lax.axis_index("layer")
    seq = lax.axis_index("seq")
    c = lax.rem(seq, 2)
    m = lax.div(seq, 2)
    y = lax.rem(m, 4)
    z = lax.div(m, 4)
    oc = 1 - c
    yp = lax.rem(y + 1, 4)
    ym = lax.rem(y + 3, 4)
    y2 = lax.rem(y + 2, 4)
    oz = 1 - z

    def at(zz, yy, cc):
        return (layer, zz * 8 + yy * 2 + cc)

    sib = at(z, y, oc)
    to_yp = at(z, yp, c)
    to_ym = at(z, ym, c)
    to_z = at(oz, y, c)
    up = (lax.rem(layer + 1, 8), seq)
    down = (lax.rem(layer + 7, 8), seq)
    after = (layer, lax.rem(seq + 2, 16))
    before = (layer, lax.rem(seq + 14, 16))

    def mult(v, by):
        return pl.multiple_of(v, by)

    local = (
        (w_in.at[pl.ds(8192, 1088), :], w_rows.at[pl.ds(8192, 1088), :]),
        (w_in.at[pl.ds(4096, 4096), :], w_rows.at[pl.ds(4096, 4096), :]),
        (w_in.at[pl.ds(0, 4096), :], w_rows.at[pl.ds(0, 4096), :]),
        (panels, hid.at[0, c]),
        (state_in.at[pl.ds(mult(c * HALF, HALF), HALF), :], s_in.at[c]),
        (w_out.at[pl.ds(mult(c * HALF, HALF), HALF), :], w_o),
        (feed.at[:, :, pl.ds(mult(c * 1024, 1024), 1024)], fd.at[:, c]),
    )
    for i, (src, dst) in enumerate(local[:3]):
        pltpu.make_async_copy(src, dst, l_sem.at[i]).start()

    barrier = pltpu.get_barrier_semaphore()
    friends = (sib, to_yp, to_ym, to_z, up, down, after, before)
    for friend in friends:
        pl.semaphore_signal(barrier, inc=1, device_id=friend, device_id_type=MESH)

    heads[...] = jnp.zeros((8, 128), F32)
    heads[0:1, 0:64] = dt_bias[...]
    heads[1:2, 0:64] = decay_rate[...]
    heads[2:3, 0:64] = skip_gain[...]
    tails[c, 0:8, :] = jnp.zeros((8, 5120), F32)
    tails[c, 5:8, :] = tail_in[...].astype(F32)

    for i, (src, dst) in enumerate(local[:3]):
        pltpu.make_async_copy(src, dst, l_sem.at[i]).wait()
    pl.semaphore_wait(barrier, len(friends))

    def remote(src, dst, ss, rs, who):
        return pltpu.make_async_remote_copy(
            src_ref=src, dst_ref=dst, send_sem=ss, recv_sem=rs, device_id=who, device_id_type=MESH
        )

    own_rows = mult(m * 256 + c * 128, 128)
    sib_rows = mult(m * 256 + oc * 128, 128)

    def turned(start, size):
        return w_rows[pl.ds(mult(start, 64), size), :].T

    def bc_prepare():
        dt = jnp.concatenate([turned(9216, 64), jnp.zeros((128, 64), BF16)], axis=1)
        rows = pl.ds(own_rows, 128)
        for cc, target, where in ((c, w_bc, rows), (oc, bc_cut, slice(0, 128))):
            target[where, 0:256] = turned(8192 + cc * 256, 256)
            target[where, 256:512] = turned(8704 + cc * 256, 256)
            target[where, 512:640] = dt
        remote(bc_cut, w_bc.at[rows, :], g_send.at[8, 18], g_recv.at[8, 18], sib).start()
        push(bc_part(m, c), 8, 2, to_z)
        push(bc_part(m, c), 8, 0, to_yp)
        push(bc_part(m, c), 8, 1, to_ym)

    def main_prepare(q):
        rows = pl.ds(own_rows, 128)
        w_main[q, rows, 0:256] = turned(4096 + c * 2048 + q * 256, 256)
        w_main[q, rows, 256:512] = turned(c * 2048 + q * 256, 256)
        w_cut[q, :, 0:256] = turned(4096 + oc * 2048 + q * 256, 256)
        w_cut[q, :, 256:512] = turned(oc * 2048 + q * 256, 256)
        remote(w_cut.at[q], w_main.at[q, rows, :], g_send.at[q, 18], g_recv.at[q, 18], sib).start()

    def bc_landed():
        return w_bc.at[pl.ds(sib_rows, 128), :]

    def main_landed(q):
        return w_main.at[q, pl.ds(sib_rows, 128), :]

    def bc_part(mm, half=None):
        if half is None:
            return w_bc.at[pl.ds(mult(mm * 256, 256), 256), :]
        return w_bc.at[pl.ds(mult(mm * 256 + half * 128, 128), 128), :]

    def main_part(q, mm, half=None):
        if half is None:
            return w_main.at[q, pl.ds(mult(mm * 256, 256), 256), :]
        return w_main.at[q, pl.ds(mult(mm * 256 + half * 128, 128), 128), :]

    def part_of(q):
        return functools.partial(main_part, q)

    m_yp, m_ym, m_y2 = z * 4 + yp, z * 4 + ym, z * 4 + y2
    o_y, o_yp, o_ym, o_y2 = oz * 4 + y, oz * 4 + yp, oz * 4 + ym, oz * 4 + y2

    def push(part, q, slot, who):
        remote(part, part, g_send.at[q, slot], g_recv.at[q, slot], who).start()

    def arrived(part, q, slot):
        remote(part, part, g_send.at[q, slot], g_recv.at[q, slot], sib).wait_recv()

    def sent(part, q, slot):
        remote(part, part, g_send.at[q, slot], g_recv.at[q, slot], sib).wait_send()

    def first_x(part, q):
        push(part(m), q, 2, to_z)
        push(part(m), q, 0, to_yp)
        push(part(m), q, 1, to_ym)

    def first_g(part, q):
        push(part(m), q, 5, to_z)
        push(part(m), q, 3, to_yp)
        push(part(m), q, 4, to_ym)

    def landed_first(part, q, mm, slot):
        if part is bc_part:
            arrived(part(mm, c), q, slot)
            arrived(part(mm, oc), q, slot + 3)
        else:
            arrived(part(mm), q, slot)

    def second_x(part, q):
        landed_first(part, q, o_y, 2)
        push(part(o_y), q, 6, to_yp)
        push(part(o_y), q, 7, to_ym)
        landed_first(part, q, m_ym, 0)
        push(part(m_ym, 0), q, 8, to_yp)
        landed_first(part, q, m_yp, 1)
        push(part(m_yp, 1), q, 9, to_ym)

    def second_g(part, q):
        arrived(part(m_ym), q, 3)
        push(part(m_ym), q, 11, to_z)
        push(part(m_ym, 0), q, 10, to_yp)
        arrived(part(m_yp), q, 4)
        push(part(m_yp), q, 13, to_z)
        push(part(m_yp, 1), q, 12, to_ym)
        arrived(part(o_y), q, 5)

    def third_x(part, q):
        arrived(part(o_ym), q, 6)
        push(part(o_ym, 0), q, 14, to_yp)
        arrived(part(o_yp), q, 7)
        push(part(o_yp, 1), q, 15, to_ym)
        arrived(part(m_y2, 0), q, 8)
        arrived(part(m_y2, 1), q, 9)

    def third_g(part, q):
        arrived(part(m_y2, 0), q, 10)
        push(part(m_y2, 0), q, 16, to_z)
        arrived(part(m_y2, 1), q, 12)
        push(part(m_y2, 1), q, 17, to_z)
        arrived(part(o_ym), q, 11)
        arrived(part(o_yp), q, 13)

    def last_x(part, q):
        arrived(part(o_y2, 0), q, 14)
        arrived(part(o_y2, 1), q, 15)

    def last_g(part, q):
        arrived(part(o_y2, 0), q, 16)
        arrived(part(o_y2, 1), q, 17)

    def sent_x(part, q):
        for slot in (0, 1, 2):
            if part is bc_part:
                sent(part(m, 0), q, slot)
                sent(part(m, 0), q, slot + 3)
            else:
                sent(part(m), q, slot)
        for slot in (6, 7):
            sent(part(m), q, slot)
        for slot in (8, 9, 14, 15):
            sent(part(m, 0), q, slot)

    def sent_g(part, q):
        for slot in (3, 4, 5, 11, 13):
            sent(part(m), q, slot)
        for slot in (10, 12, 16, 17):
            sent(part(m, 0), q, slot)

    bc_prepare()
    main_prepare(0)
    arrived(bc_landed(), 8, 18)
    push(bc_part(m, oc), 8, 5, to_z)
    push(bc_part(m, oc), 8, 3, to_yp)
    push(bc_part(m, oc), 8, 4, to_ym)

    @pl.loop(0, STEPS // 2)
    def _(i):
        q = 2 * i
        main_prepare(q + 1)
        arrived(main_landed(q), q, 18)
        first_x(part_of(q), q)

        @pl.when(i < STEPS // 2 - 1)
        def _():
            main_prepare(q + 2)

        arrived(main_landed(q + 1), q + 1, 18)
        first_g(part_of(q + 1), q + 1)

    begin = (
        (panels, hid.at[0, c], 0),
        (tails.at[c], tails.at[c], 1),
        (state_in.at[pl.ds(mult(oc * HALF, HALF), HALF), :], s_in.at[c], 2),
        (feed.at[:, :, pl.ds(mult(oc * 1024, 1024), 1024)], fd.at[:, c], 3),
    )
    for src, dst, i in begin:
        remote(src, dst, m_send.at[i], m_recv.at[i], sib).start()
    for i, (src, dst) in enumerate(local[3:]):
        pltpu.make_async_copy(src, dst, l_sem.at[3 + i]).start()
    for i, (src, dst) in enumerate(local[3:]):
        pltpu.make_async_copy(src, dst, l_sem.at[3 + i]).wait()
    for (src, dst, i), land in zip(begin, (hid.at[0, oc], tails.at[oc], s_in.at[oc], fd.at[:, oc])):
        remote(land, land, m_send.at[i], m_recv.at[i], sib).wait_recv()

    def ingest(t, tile, n):
        cols = pl.ds(mult(n * PIECE, PIECE), PIECE)
        rows = pl.ds(mult(tile * SEG, 32), SEG)
        h = hid[t, tile, :, cols].astype(F32)
        ssq[rows, :] += lane_sums(h * h)
        hg[rows, cols] = (h * norm_gain[:, cols]).astype(BF16)

    lane = lax.broadcasted_iota(jnp.int32, (SEG, 128), 1)
    row = lax.broadcasted_iota(jnp.int32, (SEG, 128), 0)

    def conv(slot, tile_tail, fresh, weight, bias):
        convbuf[slot, 0:8, :] = tile_tail
        convbuf[slot, 8 : 8 + SEG, :] = fresh
        total = bias
        for k in range(4):
            total = total + convbuf[slot, 5 + k : 5 + k + SEG, :] * weight[k : k + 1, :]
        return silu_of_half(total).astype(BF16)

    def x_tail(t, tile, q, pair, cols):
        lanes = slice(pair * 128, pair * 128 + 128)
        if t == 0:
            return tails[tile, :, cols]
        if tile == 1:
            return x_loc[t - 1, q, :, lanes]
        return jnp.where(m > 0, s_recv[t - 1, q, 128:144, lanes].astype(F32)[8:16], 0.0)

    def bc_tail(t, tile, block, cols):
        lanes = slice(block * 128, block * 128 + 128)
        if t == 0:
            return tails[tile, :, cols]
        if tile == 1:
            return bc_loc[t - 1, :, lanes]
        return jnp.where(m > 0, bc_from[t - 1, :, lanes].astype(F32)[8:16], 0.0)

    def keep_tail(t, tile, slot, here, away):
        if t < 2 and tile == 0:
            target, at_ = here
            target[at_] = convbuf[slot, SEG : SEG + 8, :]
        elif t < 2:
            target, at_ = away
            target[at_] = convbuf[slot, SEG - 8 : SEG + 8, :].astype(BF16)

    def project(tile, q, into, half):
        cols = slice(half * 256, half * 256 + 256)
        into[:, cols] = dot(hg[tile * SEG : (tile + 1) * SEG, :], w_main[q, :, cols])

    def prologue(t, tile):
        rows = slice(tile * SEG, (tile + 1) * SEG)
        if t > 0 and tile == 0:
            remote(bc_to.at[t - 1], bc_from.at[t - 1], m_send.at[3 + t], m_recv.at[3 + t], after).wait_recv()
        total = jnp.sum(ssq[rows, :], axis=1, keepdims=True)
        rowscale[rows, :] = jnp.broadcast_to(lax.rsqrt(total * (1.0 / WIDTH) + EPS), (SEG, 128))
        proj[...] = dot(hg[rows, :], w_bc[...])
        if t > 0:
            for half in range(2):
                project(tile, 0, made_a, half)
        causal = lane <= row
        tri = (
            lax.broadcasted_iota(jnp.int32, (SEG, SEG), 1) <= lax.broadcasted_iota(jnp.int32, (SEG, SEG), 0)
        ).astype(BF16)
        sq_mine[rows, :] = jnp.zeros((SEG, 128), F32)
        scale = rowscale[rows, :]
        for block in range(4):
            slot = block % 2
            base = 4096 if block < 2 else 4608
            cols = pl.ds(mult(base + c * 256 + slot * 128, 128), 128)
            fresh = proj[:, block * 128 : block * 128 + 128] * scale
            made = conv(
                tile * 2 + slot, bc_tail(t, tile, block, cols), fresh, 0.5 * conv_w[:, cols], 0.5 * conv_b[:, cols]
            )
            lanes = slice(block * 128, block * 128 + 128)
            keep_tail(t, tile, tile * 2 + slot, (bc_loc, (min(t, 1), slice(0, 8), lanes)), (bc_to, (min(t, 1), slice(0, 16), lanes)))
            target = b_all if block < 2 else c_all
            target[tile, slot] = made
        for g in range(2):
            scores = lax.dot_general(
                c_all[tile, g], b_all[tile, g], (((1,), (1,)), ((), ())), preferred_element_type=F32
            )
            score_a[tile, g] = jnp.where(causal, scores[:, 0:128], 0.0)
            score_b[tile, g] = jnp.where(causal[0:32, 0:32], scores[128:SEG, 128:SEG], 0.0)
        v = proj[:, 512:640] * scale + heads[0:1, :]
        step = jnp.maximum(v, 0.0) + jnp.log1p(jnp.exp(-jnp.abs(v)))
        fall = -heads[1:2, :] * step
        coarse = fall.astype(BF16)
        rest = fall - coarse.astype(F32)
        fine = rest.astype(BF16)
        finest = (rest - fine.astype(F32)).astype(BF16)
        sums = dot(tri, jnp.concatenate([coarse, fine, finest], axis=1))
        ld = sums[:, 0:128] + (sums[:, 128:256] + sums[:, 256:384])
        last = ld[SEG - 1 : SEG, :]
        ld_col[tile] = ld * LOG2E
        ld_row[tile, :, 0:SEG] = (ld * LOG2E - jnp.log2(step)).T
        e_all[2 * tile * SEG : (2 * tile + 1) * SEG, :] = jnp.exp(ld).astype(BF16)
        e_all[(2 * tile + 1) * SEG : (2 * tile + 2) * SEG, :] = (jnp.exp(last - ld) * step).astype(BF16)
        e_fin[tile, 0:1, :] = jnp.exp(last)
        e_fin[tile, 1:2, :] = heads[2:3, :]

        if t < 2 and tile == 1:
            remote(bc_to.at[t], bc_from.at[t], m_send.at[4 + t], m_recv.at[4 + t], after).start()

    low = lane < 64

    def state_arrived(t, q):
        land = s_recv.at[t - 1, q]
        remote(land, land, st_send.at[t - 1, q], st_recv.at[t - 1, q], after).wait_recv()

    def step_of(t, tile, q, made_of, beside):
        beside(0)
        rows = slice(tile * SEG, (tile + 1) * SEG)
        g = lax.div(q, 4)
        base = c * 32 + q * 4
        first = lax.rem(128 - base, 128)
        spread = (
            lax.broadcasted_iota(jnp.int32, (128, CHUNK), 0)
            == base + lax.div(lax.broadcasted_iota(jnp.int32, (128, CHUNK), 1), 64)
        ).astype(F32)
        both_e = slice(2 * tile * SEG, (2 * tile + 2) * SEG)
        spread_out = dot(e_all[both_e, :], spread.astype(BF16))
        scale = rowscale[rows, :]
        half_scale = 0.5 * scale
        if t == 0:
            state = s_in[tile, pl.ds(mult(q * CHUNK, CHUNK), CHUNK), :].T
        elif tile == 0:
            state = jnp.where(m > 0, s_recv[t - 1, q, 0:128, :].astype(F32), 0.0)
        else:
            state = s_loc[t - 1, q]
        ld = pltpu.roll(ld_col[tile], first, 1)
        ends = pltpu.roll(e_fin[tile], first, 1)
        sa, sb = score_a[tile, g], score_b[tile, g]
        carried = dot(c_all[tile, g], state.astype(BF16))
        squares = jnp.zeros((SEG, 128), F32)
        grown = []
        xs = []
        for pair in range(2):
            lanes = slice(pair * 128, pair * 128 + 128)
            cols = pl.ds(mult(c * HALF + q * CHUNK + pair * 128, 128), 128)
            slot = tile * 2 + pair
            x = conv(
                slot, x_tail(t, tile, q, pair, cols), made_of[:, lanes] * scale, 0.5 * conv_w[:, cols], 0.5 * conv_b[:, cols]
            )
            keep_tail(t, tile, slot, (x_loc, (min(t, 1), q, slice(0, 8), lanes)), (s_send, (min(t, 1), q, slice(128, 144), lanes)))
            xs.append(x)
        beside(1)
        for pair in range(2):
            lanes = slice(pair * 128, pair * 128 + 128)
            cols = pl.ds(mult(c * HALF + q * CHUNK + pair * 128, 128), 128)
            x = xs[pair]
            weights = []
            for h in (pair * 2, pair * 2 + 1):
                col = jnp.broadcast_to(ld[:, h : h + 1], (SEG, 128))
                ldr = ld_row[tile, pl.ds(base + h, 1), :]
                wa = (sa * jnp.exp2(jnp.minimum(col - ldr[:, 0:128], 64.0))).astype(BF16)
                wb = (sb * jnp.exp2(jnp.minimum(col[128:SEG, 0:32] - ldr[:, 128:SEG], 64.0))).astype(BF16)
                wb = jnp.concatenate([jnp.zeros((128, 32), BF16), wb], axis=0)
                weights.append(jnp.concatenate([wa, wb], axis=1))
            both = dot(jnp.concatenate(weights, axis=0), x)
            mixed = jnp.where(low, both[0:SEG], both[SEG : 2 * SEG])
            wide = x.astype(F32)
            end = jnp.where(low[0:8], ends[:, 2 * pair : 2 * pair + 1], ends[:, 2 * pair + 1 : 2 * pair + 2])
            e_now = spread_out[0:SEG, lanes]
            e_last = spread_out[SEG : 2 * SEG, lanes]
            combined = mixed + carried[:, lanes] * e_now + end[1:2, :] * wide
            gate = slice(CHUNK + pair * 128, CHUNK + pair * 128 + 128)
            out = combined * silu_of_half(made_of[:, gate] * half_scale)
            squares = squares + out * out
            gated[rows, pl.ds(mult(q * CHUNK + pair * 128, 128), 128)] = (out * out_gain[:, cols]).astype(BF16)
            grew = lax.dot_general(
                b_all[tile, g], (wide * e_last).astype(BF16), (((0,), (0,)), ((), ())), preferred_element_type=F32
            )
            grown.append(end[0:1, :] * state[:, lanes] + grew)
        sq_mine[rows, :] += squares
        made = jnp.concatenate(grown, axis=1)
        if t < 2 and tile == 0:
            s_loc[t, q] = made
        elif t < 2:
            s_send[t, q, 0:128, :] = made.astype(BF16)
        else:
            s_in[tile, pl.ds(mult(q * CHUNK, CHUNK), CHUNK), :] = made.T

    def state_off(t, tile, q):
        if t < 2 and tile == 1:
            remote(s_send.at[t, q], s_recv.at[t, q], st_send.at[t, q], st_recv.at[t, q], after).start()
        elif t == 2:
            place = state_out.at[pl.ds(mult(c * HALF + q * CHUNK, CHUNK), CHUNK), :]
            turned_q = pl.ds(mult(q * CHUNK, CHUNK), CHUNK)

            @pl.when(c == tile)
            def _():
                pltpu.make_async_copy(s_in.at[tile, turned_q, :], place, f_loc.at[q]).start()

            @pl.when(c != tile)
            def _():
                remote(s_in.at[tile, turned_q, :], place, f_send.at[q], f_recv.at[q], sib).start()

    def piece_cols(half, p):
        return pl.ds(mult(half * 1024 + p * PIECE, PIECE), PIECE)

    def panel_off(t, tile, p):
        there = hid.at[t + 1, tile, :, piece_cols(c, p)]
        remote(pan_send.at[t, tile, p], there, n_send.at[t, tile, p], n_recv.at[t, tile, p], up).start()

    def emit(t, tile):
        rows = slice(tile * SEG, (tile + 1) * SEG)
        sq_send[t, tile] = sq_mine[rows, :]
        remote(sq_send.at[t, tile], sq_recv.at[t, tile], q_send.at[t, tile], q_recv.at[t, tile], sib).start()

        for p in range(2):
            part_send[t, tile, p] = dot(gated[rows, :], w_o[:, piece_cols(oc, p)]).astype(BF16)
            remote(
                part_send.at[t, tile, p], part_recv.at[t, tile, p], p_send.at[t, tile, p], p_recv.at[t, tile, p], sib
            ).start()

        own_part[0] = dot(gated[rows, :], w_o[:, piece_cols(c, 0)])

        if (t, tile) == (1, 0):
            relay(1, 1)
        remote(sq_recv.at[t, tile], sq_recv.at[t, tile], q_send.at[t, tile], q_recv.at[t, tile], sib).wait_recv()
        squares = jnp.sum(sq_mine[rows, :] + sq_recv[t, tile], axis=1, keepdims=True)
        scale = jnp.broadcast_to(lax.rsqrt(squares * (1.0 / 4096) + EPS), (SEG, 128))
        for p in range(2):
            land = part_recv.at[t, tile, p]
            remote(land, land, p_send.at[t, tile, p], p_recv.at[t, tile, p], sib).wait_recv()
            if p == 1:
                own_part[1] = dot(gated[rows, :], w_o[:, piece_cols(c, 1)])
            whole = own_part[p] + part_recv[t, tile, p].astype(F32)
            cols = piece_cols(c, p)
            panel = hid[t, tile, :, cols].astype(F32) + by_rows(whole, scale)
            if t < 2:
                entering = fd[t, tile, :, p * PIECE : (p + 1) * PIECE].astype(F32)
                pan_send[t, tile, p] = jnp.where(layer == 7, entering, panel).astype(BF16)
                if (t, tile) != (0, 1):
                    panel_off(t, tile, p)
            else:
                pan_stage[tile, p] = panel.astype(BF16)

                @pl.when(c == tile)
                def _():
                    pltpu.make_async_copy(pan_stage.at[tile, p], panel_out.at[:, cols], o_loc.at[p]).start()

                @pl.when(c != tile)
                def _():
                    remote(pan_stage.at[tile, p], panel_out.at[:, cols], o_send.at[p], o_recv.at[p], sib).start()

    def relay(t, tile):
        for p in range(2):
            part = hid.at[t, tile, :, piece_cols(c, p)]
            remote(part, part, n_send.at[t - 1, tile, p], n_recv.at[t - 1, tile, p], up).wait_recv()
            remote(part, part, r_send.at[t - 1, tile, p], r_recv.at[t - 1, tile, p], sib).start()

    def receive(t, tile):
        for p in range(2):
            ingest(t, tile, c * 2 + p)
        for p in range(2):
            part = hid.at[t, tile, :, piece_cols(oc, p)]
            remote(part, part, r_send.at[t - 1, tile, p], r_recv.at[t - 1, tile, p], sib).wait_recv()
            ingest(t, tile, oc * 2 + p)

    ssq[...] = jnp.zeros((2 * SEG, 128), F32)

    @pl.loop(0, 2 * PIECES)
    def _(i):
        ingest(0, lax.rem(i, 2), lax.div(i, 2))

    second_x(bc_part, 8)

    @pl.loop(0, STEPS // 2)
    def _(i):
        second_x(part_of(2 * i), 2 * i)
        second_g(part_of(2 * i + 1), 2 * i + 1)

    third_x(bc_part, 8)

    @pl.loop(0, STEPS // 2)
    def _(i):
        third_x(part_of(2 * i), 2 * i)
        third_g(part_of(2 * i + 1), 2 * i + 1)

    last_x(bc_part, 8)
    for tile in range(2):
        prologue(0, tile)

    @pl.loop(0, STEPS - 1)
    def _(q):
        @pl.when(lax.rem(q, 2) == 0)
        def _():
            last_x(part_of(q), q)

        @pl.when(lax.rem(q, 2) == 1)
        def _():
            last_g(part_of(q), q)

        for half in range(2):
            project(0, q, made_a, half)
        step_of(0, 0, q, made_a, functools.partial(project, 1, q, made_b))
        step_of(0, 1, q, made_b, lambda half: None)
        state_off(0, 1, q)

    last_g(part_of(STEPS - 1), STEPS - 1)
    for tile in range(2):
        for half in range(2):
            project(tile, STEPS - 1, made_a, half)
        step_of(0, tile, STEPS - 1, made_a, lambda half: None)
        state_off(0, tile, STEPS - 1)
        emit(0, tile)

    for t in (1, 2):
        for tile in range(2):
            ssq[tile * SEG : (tile + 1) * SEG, :] = jnp.zeros((SEG, 128), F32)
            if (t, tile) != (1, 1):
                relay(t, tile)
            if (t, tile) == (1, 0):
                for p in range(2):
                    panel_off(0, 1, p)
            receive(t, tile)
            prologue(t, tile)

            @pl.loop(0, STEPS // 2)
            def _(i):
                q = 2 * i
                if tile == 0:
                    state_arrived(t, q)
                    state_arrived(t, q + 1)
                step_of(t, tile, q, made_a, functools.partial(project, tile, q + 1, made_b))
                step_of(t, tile, q + 1, made_b, functools.partial(project, tile, lax.rem(q + 2, STEPS), made_a))
                state_off(t, tile, q)
                state_off(t, tile, q + 1)

            emit(t, tile)

    sent(bc_landed(), 8, 18)
    sent_x(bc_part, 8)

    @pl.loop(0, STEPS)
    def _(q):
        sent(main_landed(q), q, 18)

        @pl.when(lax.rem(q, 2) == 0)
        def _():
            sent_x(part_of(q), q)

        @pl.when(lax.rem(q, 2) == 1)
        def _():
            sent_g(part_of(q), q)

        place = state_out.at[pl.ds(mult(c * HALF + q * CHUNK, CHUNK), CHUNK), :]
        land = state_out.at[pl.ds(mult(oc * HALF + q * CHUNK, CHUNK), CHUNK), :]
        turned_q = pl.ds(mult(q * CHUNK, CHUNK), CHUNK)
        pltpu.make_async_copy(s_in.at[c, turned_q, :], place, f_loc.at[q]).wait()
        remote(s_in.at[oc, turned_q, :], land, f_send.at[q], f_recv.at[q], sib).wait()
        for t in range(2):
            remote(s_send.at[t, q], s_recv.at[t, q], st_send.at[t, q], st_recv.at[t, q], after).wait_send()

    for src, dst, i in begin:
        remote(src, dst, m_send.at[i], m_recv.at[i], sib).wait_send()
    for t in range(2):
        remote(bc_to.at[t], bc_from.at[t], m_send.at[4 + t], m_recv.at[4 + t], after).wait_send()

    for p in range(2):
        pltpu.make_async_copy(pan_stage.at[c, p], panel_out.at[:, piece_cols(c, p)], o_loc.at[p]).wait()
        remote(pan_stage.at[oc, p], panel_out.at[:, piece_cols(oc, p)], o_send.at[p], o_recv.at[p], sib).wait()

    @pl.loop(0, 2)
    def _(tile):
        for t in range(3):
            remote(sq_send.at[t, tile], sq_recv.at[t, tile], q_send.at[t, tile], q_recv.at[t, tile], sib).wait_send()
            for p in range(2):
                src, dst = part_send.at[t, tile, p], part_recv.at[t, tile, p]
                remote(src, dst, p_send.at[t, tile, p], p_recv.at[t, tile, p], sib).wait_send()
        for t in range(2):
            for p in range(2):
                part = hid.at[t + 1, tile, :, piece_cols(c, p)]
                remote(pan_send.at[t, tile, p], part, n_send.at[t, tile, p], n_recv.at[t, tile, p], up).wait_send()
                remote(part, part, r_send.at[t, tile, p], r_recv.at[t, tile, p], sib).wait_send()


def hand_over(panel, state, panel_out, state_out, panel_here, state_here, sem_in, sem_out):
    pieces = [(panel, panel_here, panel_out)]
    for i in range(4):
        rows = pl.ds(i * 1024, 1024)
        pieces.append((state.at[rows, :], state_here.at[rows, :], state_out.at[rows, :]))
    for i, (src, here, _) in enumerate(pieces):
        pltpu.make_async_copy(src, here, sem_in.at[i]).start()
    for i, (src, here, dst) in enumerate(pieces):
        pltpu.make_async_copy(src, here, sem_in.at[i]).wait()
        pltpu.make_async_copy(here, dst, sem_out.at[i]).start()
    for i, (_, here, dst) in enumerate(pieces):
        pltpu.make_async_copy(here, dst, sem_out.at[i]).wait()


def local(
    panels, feed, ssm_state, conv_state, w_in, w_out, norm_gain, conv_weight, conv_bias,
    dt_bias, decay_rate, skip_gain, out_gain,
):
    any_ = pl.BlockSpec(memory_space=pl.ANY)
    vmem = pl.BlockSpec(memory_space=pltpu.VMEM)
    dma = pltpu.SemaphoreType.DMA
    scratch = [
        pltpu.VMEM((9280, 128), BF16),
        pltpu.VMEM((STEPS, 128, 512), BF16),
        pltpu.VMEM((128, 640), BF16),
        pltpu.VMEM((8, 128), F32),
        pltpu.VMEM((STEPS, 2048, 512), BF16),
        pltpu.VMEM((2048, 640), BF16),
        pltpu.VMEM((HALF, WIDTH), BF16),
        pltpu.VMEM((3, 2, SEG, WIDTH), BF16),
        pltpu.VMEM((2 * SEG, WIDTH), BF16),
        pltpu.VMEM((2 * SEG, 128), F32),
        pltpu.VMEM((2 * SEG, 128), F32),
        pltpu.VMEM((2, 8, 5120), F32),
        pltpu.VMEM((2, STEPS, 8, CHUNK), F32),
        pltpu.VMEM((2, 8, 512), F32),
        pltpu.VMEM((2, 16, 512), BF16),
        pltpu.VMEM((2, 16, 512), BF16),
        pltpu.VMEM((2, HALF, 128), F32),
        pltpu.VMEM((2, STEPS, 128, CHUNK), F32),
        pltpu.VMEM((2, STEPS, 144, CHUNK), BF16),
        pltpu.VMEM((2, STEPS, 144, CHUNK), BF16),
        pltpu.VMEM((2, 2, SEG, 1024), BF16),
        pltpu.VMEM((4, SEG + 8, 128), F32),
        pltpu.VMEM((SEG, 640), F32),
        pltpu.VMEM((SEG, 512), F32),
        pltpu.VMEM((SEG, 512), F32),
        pltpu.VMEM((2, 2, SEG, 128), BF16),
        pltpu.VMEM((2, 2, SEG, 128), BF16),
        pltpu.VMEM((2, 2, SEG, 128), F32),
        pltpu.VMEM((2, 2, 32, 32), F32),
        pltpu.VMEM((2, SEG, 128), F32),
        pltpu.VMEM((2, 128, 256), F32),
        pltpu.VMEM((4 * SEG, 128), BF16),
        pltpu.VMEM((2, 8, 128), F32),
        pltpu.VMEM((2 * SEG, HALF), BF16),
        pltpu.VMEM((2, SEG, PIECE), F32),
        pltpu.VMEM((3, 2, 2, SEG, PIECE), BF16),
        pltpu.VMEM((3, 2, 2, SEG, PIECE), BF16),
        pltpu.VMEM((2 * SEG, 128), F32),
        pltpu.VMEM((3, 2, SEG, 128), F32),
        pltpu.VMEM((3, 2, SEG, 128), F32),
        pltpu.VMEM((2, 2, 2, SEG, PIECE), BF16),
        pltpu.VMEM((2, 2, SEG, PIECE), BF16),
        dma((9, 19)), dma((9, 19)), dma((7,)), dma((6,)), dma((6,)), dma((3, 2, 2)), dma((3, 2, 2)),
        dma((2, 2, 2)), dma((2, 2, 2)), dma((2, 2, 2)), dma((2, 2, 2)),
        dma((2, STEPS)), dma((2, STEPS)), dma((STEPS,)), dma((STEPS,)), dma((STEPS,)),
        dma((3, 2)), dma((3, 2)), dma((2,)), dma((2,)), dma((2,)),
    ]
    panel, state = pl.pallas_call(
        kernel,
        out_shape=(
            jax.ShapeDtypeStruct((SEG, WIDTH), BF16),
            jax.ShapeDtypeStruct((4096, 128), F32),
        ),
        in_specs=[any_] * 5 + [vmem] * 8,
        out_specs=(any_, any_),
        scratch_shapes=scratch,
        compiler_params=pltpu.CompilerParams(
            collective_id=0, has_side_effects=True, vmem_limit_bytes=60 * 1024 * 1024
        ),
        cost_estimate=pl.CostEstimate(flops=28_000_000_000, bytes_accessed=60_000_000, transcendentals=20_000_000),
    )(
        panels[0], feed, ssm_state.reshape(4096, 128), w_in[0].T, w_out[0], conv_state[0, 0],
        norm_gain, conv_weight[0], conv_bias, dt_bias, decay_rate, skip_gain, out_gain,
    )
    panel, state = pl.pallas_call(
        hand_over,
        out_shape=(jax.ShapeDtypeStruct((SEG, WIDTH), BF16), jax.ShapeDtypeStruct((4096, 128), F32)),
        in_specs=[any_, any_],
        out_specs=(any_, any_),
        scratch_shapes=[pltpu.VMEM((SEG, WIDTH), BF16), pltpu.VMEM((4096, 128), F32), dma((5,)), dma((5,))],
        compiler_params=pltpu.CompilerParams(vmem_limit_bytes=60 * 1024 * 1024),
    )(panel, state)
    return (panel[None], state.reshape(1, 1, 64, 64, 128))


def solution(mesh):
    return jax.shard_map(
        local,
        mesh=mesh,
        in_specs=(
            P("layer", "seq", None),
            P(None, "seq", None),
            P("layer", "seq", None, None, None),
            P("layer", "seq", None, None),
            P("layer", "seq", None),
            P("layer", None, None),
            P("layer", None),
            P("layer", None, None),
            P("layer", None),
            P("layer", None),
            P("layer", None),
            P("layer", None),
            P("layer", None),
        ),
        out_specs=(P("layer", "seq", None), P("layer", "seq", None, None, None)),
        check_vma=False,
    )
```
